512 devices in a mesh: tensor: 8 (over y, core), vocab: 64 (over z, x).
Axes of the slice: x: 4, y: 4, z: 16, core: 2. Of those that a mesh axis runs over, the one named last changes fastest.
Arguments:
- partials: bfloat16 [3, 8, 256, 4096], P(None, 'tensor', 'vocab'), may hold values from -256 to 256
- norm_gain: bfloat16 [4096], replicated, may hold values from 0.5 to 1.5
- head_weight: bfloat16 [4096, 131072], P(None, ('tensor', 'vocab')), may hold values from -0.7861328 to 0.7861328
- draft_ids: int32 [3, 256], replicated, may hold values from 0 to 131071
- tree_parents: int32 [256], replicated, may hold values from 0 to 62, as said below
- accepted_lengths: int32 [3, 4], replicated, may hold values from 1 to 5
Outputs:
- probabilities: bfloat16 [3, 256, 131072], P(None, None, ('tensor', 'vocab'))
- entropy: float32 [3, 256], replicated
- typical_margin: float32 [3, 256], replicated
- path_score: float32 [3, 4], replicated
The draws below stay inside these ranges and needn't reach their ends.
Inputs may be any that keep to these rules, and one draw needn't show every extreme that they name: `tree_parents`: each row names an earlier row of its own tree of 64 rows by its position in the tree; a tree's first row names itself.
All inputs are finite; a program needn't handle non-finite values.
Results may differ from the reference program's by a relative error of at most 0.009.
Values may be sent and summed in bfloat16 or wider, within the bound.
A program may use at most 64 MiB of HBM per device.

```python
import math
import jax
import jax.numpy as jnp
import numpy as np
from jax import lax

D = 4096
V = 131072
HBLOCK = 128
NODES = 64
ACCEPT_MAX = 5
ROUNDS = 3
ROWS = 256
TREES = 4
N_TENSOR = 8


def draw_partials(key, part):
    key = jax.random.fold_in(key, 3)
    keys = jax.random.split(key, 3)
    shape = (ROUNDS, N_TENSOR, ROWS, D)
    feature = jnp.arange(D, dtype=jnp.float32)
    rise = jnp.exp(0.5 * math.log(3.0) * feature / D)
    rough = jnp.exp(jax.random.uniform(keys[1], (D,), jnp.float32, math.log(0.5), math.log(2.0)))
    base = jax.random.truncated_normal(keys[0], -6.0, 6.0, shape, jnp.float32)
    row_scale = jnp.exp(jax.random.uniform(keys[2], (ROUNDS, N_TENSOR, ROWS, 1), jnp.float32, 0.0, math.log(10.0)))
    values = base * row_scale * rise * rough
    return values.astype(jnp.bfloat16)


def draw_head_weight(key, part):
    key = jax.random.fold_in(key, 5)
    keys = jax.random.split(key, 2)
    column = jnp.arange(V, dtype=jnp.float32)
    scale = jnp.exp(jax.random.uniform(keys[1], (V,), jnp.float32, math.log(0.4), math.log(2.5)))
    scale = scale * jnp.exp(math.log(1.1) * column / V) / math.sqrt(D)
    values = jax.random.truncated_normal(keys[0], -6.0, 6.0, (D, V), jnp.float32) * scale
    return values.astype(jnp.bfloat16)


def draw_tree_parents(key, part):
    key = jax.random.fold_in(key, 7)
    position = jnp.arange(ROWS, dtype=jnp.int32) % NODES
    parent = jax.random.randint(key, (ROWS,), 0, jnp.maximum(position, 1))
    parent = jnp.where(position == 0, 0, parent)
    parent = jnp.where(position == NODES - 1, NODES - 2, parent)
    return parent.astype(jnp.int32)


def draw_accepted_lengths(key, part):
    key = jax.random.fold_in(key, 9)
    keys = jax.random.split(key, 3)
    slot_count = ROUNDS * TREES
    lengths = jax.random.randint(keys[0], (slot_count,), 1, ACCEPT_MAX + 1)
    low_spot = jax.random.randint(keys[1], (), 0, slot_count)
    high_spot = (low_spot + 1 + jax.random.randint(keys[2], (), 0, slot_count - 1)) % slot_count
    slots = jnp.arange(slot_count, dtype=jnp.int32)
    lengths = jnp.where(slots == low_spot, 1, lengths)
    lengths = jnp.where(slots == high_spot, ACCEPT_MAX, lengths)
    return lengths.reshape(ROUNDS, TREES).astype(jnp.int32)


def with_ends(values, stream_key, low, high):
    shape = values.shape
    spot = [jax.random.randint(jax.random.fold_in(stream_key, axis), (), 0, shape[axis]) for axis in range(len(shape))]
    values = values.at[tuple(spot)].set(low)
    longest = shape.index(max(shape))
    spot[longest] = (spot[longest] + 1) % shape[longest]
    return values.at[tuple(spot)].set(high)


def ranked_wide(stream_key, shape, number_of, slope):
    portions = [min(1 << octave, number_of + 1 - (1 << octave)) * (1 << 20) // math.isqrt((1 << octave) ** slope) + 1 for octave in range((number_of + 1).bit_length()) if 1 << octave <= number_of]
    scale = 1 + sum(portions) // (1 << 30)
    grid = np.cumsum(np.array([max(1, weight // scale) for weight in portions]))
    pick = jax.random.randint(jax.random.fold_in(stream_key, 1), shape, 0, int(grid[len(portions) - 1]))
    start = jnp.left_shift(1, jnp.searchsorted(jnp.asarray(grid, jnp.int32), pick, side="right").astype(jnp.int32))
    rank = start - 1 + jax.random.randint(jax.random.fold_in(stream_key, 4), shape, 0, 1 << 30) % jnp.minimum(start, number_of + 1 - start)
    return jax.random.permutation(jax.random.fold_in(stream_key, 2), number_of)[rank].astype(jnp.int32)


def setup_inputs(seed: int = 0) -> dict:
    arg_keys = jax.random.split(jax.random.key(seed), 7)
    return {
        "partials": draw_partials(jax.random.fold_in(arg_keys[6], 71), 0),
        "norm_gain": jnp.clip(1.0 + 0.1 * jax.random.normal(arg_keys[1], (D,), jnp.float32), 0.5, 1.5).astype(jnp.bfloat16),
        "head_weight": draw_head_weight(jax.random.fold_in(arg_keys[6], 71), 0),
        "draft_ids": with_ends(ranked_wide(arg_keys[3], (ROUNDS, ROWS), V, 2), jax.random.fold_in(arg_keys[3], 3), 0, V - 1).astype(jnp.int32),
        "tree_parents": draw_tree_parents(jax.random.fold_in(arg_keys[6], 71), 0),
        "accepted_lengths": draw_accepted_lengths(jax.random.fold_in(arg_keys[6], 71), 0),
    }


norm_eps = 1e-06
typical_alpha = 0.3

def hadamard_table(size):
    index = jnp.arange(size, dtype=jnp.int32)
    common = index[:, None] & index[None, :]
    parity = jnp.zeros((size, size), jnp.int32)
    for shift_bit in range(max(size.bit_length(), 1)):
        parity = parity + (jnp.right_shift(common, shift_bit) & 1)
    signs = (1 - 2 * (parity % 2)).astype(jnp.float32)
    return signs / jnp.sqrt(jnp.float32(size))

def rotate_blocks(normed, table):
    count, width = normed.shape
    block = table.shape[0]
    blocks = normed.reshape(count, width // block, block)
    turned = jnp.einsum('rbk,kj->rbj', blocks, table, precision=lax.Precision.HIGHEST)
    return turned.reshape(count, width).astype(jnp.bfloat16)

def tree_depth(tree_parents):
    parents = tree_parents.reshape(-1, NODES).astype(jnp.int32)
    depth = jnp.broadcast_to((jnp.arange(NODES) > 0).astype(jnp.int32), parents.shape)
    for jump in range(NODES.bit_length()):
        depth = depth + jnp.take_along_axis(depth, parents, axis=1)
        parents = jnp.take_along_axis(parents, parents, axis=1)
    return depth

def reference(partials, norm_gain, head_weight, draft_ids, tree_parents, accepted_lengths):
    table = hadamard_table(HBLOCK)
    depth = tree_depth(tree_parents)
    row_index = jnp.arange(ROWS, dtype=jnp.int32)
    parent_row = (row_index // NODES * NODES + tree_parents).astype(jnp.int32)
    gain = norm_gain.astype(jnp.float32)
    prob_list = []
    entropy_list = []
    margin_list = []
    score_list = []
    for round_index in range(ROUNDS):
        hidden = lax.optimization_barrier(jnp.sum(partials[round_index].astype(jnp.float32), axis=0))
        mean_square = lax.optimization_barrier(jnp.mean(hidden * hidden, axis=1, keepdims=True))
        normed = hidden * lax.rsqrt(mean_square + norm_eps) * gain
        rotated = rotate_blocks(normed, table)
        logits = jnp.dot(rotated, head_weight, preferred_element_type=jnp.float32)
        row_max = lax.optimization_barrier(jnp.max(logits, axis=1))
        shifted = logits - row_max[:, None]
        weights = jnp.exp(shifted)
        totals = lax.optimization_barrier(jnp.sum(weights, axis=1))
        spread = lax.optimization_barrier(jnp.sum(weights * shifted, axis=1))
        prob_list.append((weights / totals[:, None]).astype(jnp.bfloat16))
        entropy = jnp.log(totals) - spread / totals
        picked = logits[parent_row, draft_ids[round_index]]
        log_draft = picked - row_max[parent_row] - jnp.log(totals[parent_row])
        margin = log_draft + entropy[parent_row] - math.log(typical_alpha)
        survive = depth < accepted_lengths[round_index][:, None]
        chosen = jnp.where(survive, log_draft.reshape(-1, NODES), jnp.float32(0.0))
        counted = lax.optimization_barrier(jnp.sum(survive.astype(jnp.float32), axis=1))
        score = lax.optimization_barrier(jnp.sum(chosen, axis=1)) / counted
        entropy_list.append(entropy)
        margin_list.append(margin)
        score_list.append(score)
    return (jnp.stack(prob_list), jnp.stack(entropy_list), jnp.stack(margin_list), jnp.stack(score_list))
```

```python
import math

import jax
import jax.numpy as jnp
from jax import lax
from jax.experimental import pallas as pl
from jax.experimental.pallas import tpu as pltpu
from jax.sharding import PartitionSpec as P

MESH = pl.DeviceIdType.MESH
HIGHEST = lax.Precision.HIGHEST
F32 = jnp.float32
BF16 = jnp.bfloat16

X = 4
Y = 4
Z = 16
PLANE = 32
KHALF = 2048
COLS = 256
ROUNDS = 3
NODES = 64
norm_eps = 1e-06
typical_alpha = 0.3


def dot(a, b, precision=None):
    return jnp.dot(a, b, precision=precision, preferred_element_type=F32)


def iota(shape, dim):
    return lax.broadcasted_iota(jnp.int32, shape, dim)


def kernel(
    partials,
    gain,
    weight,
    draft,
    parents,
    accepted,
    prob,
    entropy_out,
    margin_out,
    score_out,
    wbuf,
    rs_send,
    rs_recv,
    ss_send,
    ss_recv,
    xg,
    lp,
    lr,
    lf,
    quant,
    st_send,
    st_plane,
    st_mid,
    st_z,
    st_own,
    st_sib,
    psend,
    w_sem,
    rs_sem,
    ss_sem,
    z_sem,
    zs_sem,
    p1_sem,
    p1s_sem,
    p2_sem,
    p2s_sem,
    l_sem,
    ls_sem,
    sp_sem,
    sz_sem,
    sb_sem,
    pr_sem,
):
    t = lax.axis_index("tensor")
    v = lax.axis_index("vocab")
    x = lax.rem(v, X)
    z = lax.div(v, X)
    y = lax.div(t, 2)
    c = lax.rem(t, 2)
    sib = 1 - c

    def dev(dx, dy, dz, dc):
        return (dy * 2 + dc, dz * X + dx)

    def wait(ref, sem):
        pltpu.make_async_copy(ref, ref, sem).wait()

    def send(src, dst, ssem, rsem, device):
        pltpu.make_async_remote_copy(
            src_ref=src,
            dst_ref=dst,
            send_sem=ssem,
            recv_sem=rsem,
            device_id=device,
            device_id_type=MESH,
        ).start()

    me = c * 16 + x * Y + y

    def plane_dev(j):
        return dev(lax.div(lax.rem(j, 16), Y), lax.rem(j, Y), z, lax.div(j, 16))

    def offset(k):
        half = lax.div(k + 1, 2)
        return lax.rem(k, 2) * 2 * half - half

    def zmate(o):
        return lax.rem(z + o + Z, Z)

    barrier = pltpu.get_barrier_semaphore()

    def greet_plane(i, carry):
        j = lax.rem(me + i, PLANE)
        pl.semaphore_signal(barrier, inc=1, device_id=plane_dev(j), device_id_type=MESH)
        return carry

    def greet_z(i, carry):
        pl.semaphore_signal(
            barrier, inc=1, device_id=dev(x, y, zmate(i), c), device_id_type=MESH
        )
        return carry

    lax.fori_loop(1, PLANE, greet_plane, 0)
    lax.fori_loop(1, Z, greet_z, 0)

    own_w = pltpu.make_async_copy(
        weight.at[pl.ds(c * KHALF, KHALF)], wbuf.at[c], w_sem.at[0]
    )
    own_w.start()

    rows = [partials[r, 0].astype(F32) for r in range(ROUNDS)]
    slab = jnp.concatenate(rows + [jnp.zeros_like(rows[0])], axis=0).astype(BF16)
    for j in range(PLANE):
        rs_send[j] = slab[:, j * 128 : (j + 1) * 128]

    pl.semaphore_wait(barrier, PLANE - 1 + Z - 1)

    def rs_start(i, carry):
        j = lax.rem(me + i, PLANE)
        send(rs_send.at[j], rs_recv.at[me], rs_sem.at[0], rs_sem.at[1], plane_dev(j))
        return carry

    lax.fori_loop(1, PLANE, rs_start, 0)
    rs_recv[me] = rs_send[me]

    swap_w = pltpu.make_async_remote_copy(
        src_ref=weight.at[pl.ds(sib * KHALF, KHALF)],
        dst_ref=wbuf.at[c],
        send_sem=w_sem.at[1],
        recv_sem=w_sem.at[2],
        device_id=dev(x, y, z, sib),
        device_id_type=MESH,
    )

    common = iota((128, 128), 0) & iota((128, 128), 1)
    parity = jnp.zeros((128, 128), jnp.int32)
    for bit in range(7):
        parity = parity + (lax.shift_right_logical(common, bit) & 1)
    signs = (1 - 2 * (parity & 1)).astype(F32)

    parent_row = lax.div(iota((1, 256), 1), NODES) * NODES + parents[...]
    jump = (iota((256, 256), 0) == parent_row).astype(BF16)
    depth = jnp.broadcast_to(
        (lax.rem(iota((1, 256), 1), NODES) > 0).astype(F32), (8, 256)
    )
    for step in range(NODES.bit_length()):
        depth = depth + dot(depth.astype(BF16), jump)
        if step < NODES.bit_length() - 1:
            jump = dot(jump, jump).astype(BF16)

    gain_row = gain[me]

    wait(rs_recv.at[pl.ds(0, PLANE - 1)], rs_sem.at[1])
    swap_w.start()

    pieces = []
    for dx in range(X):
        total = jnp.zeros((16, 128), F32)
        for dy in range(Y):
            for dc in range(2):
                total = total + rs_recv[dc * 16 + dx * Y + dy].astype(F32)
        pieces.append(total)
    hidden = jnp.concatenate(
        [pieces[dx][4 * r : 4 * r + 4] for r in range(ROUNDS) for dx in range(X)],
        axis=0,
    )
    square = jnp.concatenate([hidden * hidden, jnp.zeros((80, 128), F32)], axis=0)
    ss_send[...] = jnp.broadcast_to(
        jnp.sum(square.T, axis=0, keepdims=True), (8, 128)
    )

    def ss_start(i, carry):
        j = lax.rem(me + i, PLANE)
        send(ss_send, ss_recv.at[me], ss_sem.at[0], ss_sem.at[1], plane_dev(j))
        return carry

    lax.fori_loop(1, PLANE, ss_start, 0)
    ss_recv[me] = ss_send[...]
    wait(ss_recv.at[pl.ds(0, PLANE - 1)], ss_sem.at[1])
    sums = ss_recv[0]
    for j in range(1, PLANE):
        sums = sums + ss_recv[j]
    scale = lax.rsqrt(sums[0:1] * (1.0 / 4096.0) + norm_eps)
    scale = jnp.broadcast_to(scale, (128, 128)).T[0:48]
    normed = hidden * scale * gain_row
    rotated = dot(normed, signs, HIGHEST) * (1.0 / math.sqrt(128.0))
    xg[x, y, z] = rotated.astype(BF16)

    def z_start(k, carry):
        send(
            xg.at[x, y, z],
            xg.at[x, y, z],
            zs_sem.at[0],
            z_sem.at[k],
            dev(x, y, zmate(-offset(k)), c),
        )
        return carry

    def across(k, order):
        zs = zmate(offset(k))
        chunk = xg.at[x, y, zs]

        def step(i, carry):
            target = (
                dev(lax.rem(x + i, X), y, z, c)
                if order == 0
                else dev(x, lax.rem(y + i, Y), z, c)
            )
            send(chunk, chunk, p1s_sem.at[0], p1_sem.at[k], target)
            return carry

        lax.fori_loop(1, 4, step, 0)

    def along(k, order):
        zs = zmate(offset(k))
        wait(xg.at[0, pl.ds(0, 3), 0], p1_sem.at[k])
        line = xg.at[:, y, zs] if order == 0 else xg.at[x, :, zs]

        def step(i, carry):
            target = (
                dev(x, lax.rem(y + i, Y), z, c)
                if order == 0
                else dev(lax.rem(x + i, X), y, z, c)
            )
            send(line, line, p2s_sem.at[0], p2_sem.at[k], target)
            return carry

        lax.fori_loop(1, 4, step, 0)

    across(0, 0)
    lax.fori_loop(1, Z, z_start, 0)

    def z_wait(k):
        wait(xg.at[0, 0, 0], z_sem.at[k])

    z_wait(1)
    across(1, 1)

    def forward(i, carry):
        k = 2 * i
        z_wait(k)
        across(k, 0)
        along(k - 2, 0)
        z_wait(k + 1)
        across(k + 1, 1)
        along(k - 1, 1)
        return carry

    same = lax.rem(z + c, 2)
    first_own, second_own = same, 3 - same
    first_sib, second_sib = 1 - same, 2 + same

    def head(g, carry):
        chunks = []
        for i in range(4):
            k = 4 * g + i
            wait(xg.at[pl.ds(0, 3), :, 0], p2_sem.at[k])
        for i in range(4):
            zs = zmate(offset(4 * g + i))
            chunks.append(
                jnp.concatenate(
                    [xg[dx, dy, zs] for dx in range(X) for dy in range(Y)], axis=1
                )
            )
        lhs = jnp.concatenate(chunks, axis=0)
        for cc in range(2):
            out = dot(lhs, wbuf[cc])
            for i in range(4):
                zs = zmate(offset(4 * g + i))
                lp[zs, :, cc * COLS : (cc + 1) * COLS] = out[48 * i : 48 * i + 48]
        for pos in (first_sib, second_sib):
            zs = zmate(offset(4 * g + pos))
            send(
                lp.at[zs],
                lr.at[lax.div(zs, 2)],
                ls_sem.at[0],
                l_sem.at[g],
                dev(x, y, z, sib),
            )
        return carry

    def stats(g, carry):
        wait(lr.at[pl.ds(0, 2)], l_sem.at[g])
        lane = iota((48, 128), 1)
        for pos in (first_own, second_own):
            zs = zmate(offset(4 * g + pos))
            zi = lax.div(zs, 2)
            full = lp[zs] + lr[zi]
            top = jnp.max(full, axis=1, keepdims=True)
            shifted = full - top
            weights = jnp.exp(shifted)
            total = jnp.sum(weights, axis=1, keepdims=True)
            spread = jnp.sum(weights * shifted, axis=1, keepdims=True)
            packed = jnp.where(lane == 0, top, jnp.where(lane == 1, total, spread))
            for r in range(ROUNDS):
                lf[r, zi] = full[16 * r : 16 * r + 16]
                quant[r, zi] = packed[16 * r : 16 * r + 16]
        return carry

    own_w.wait()
    swap_w.wait_recv()
    lax.fori_loop(1, 8, forward, 0)
    along(14, 0)
    along(15, 1)
    lax.fori_loop(0, 4, head, 0)
    lax.fori_loop(0, 4, stats, 0)

    def held(index, core):
        return (lax.div(index, 16) * 2 + core) * 16 + lax.rem(index, 16)

    own_parent = (held(iota((128, 256), 0), c) == parent_row).astype(F32)
    column = iota((512, 256), 0)
    column = (
        ((y * 2 + lax.div(column, COLS)) * (X * Z) + v) * COLS + lax.rem(column, COLS)
    )
    st_send[...] = jnp.zeros((16, 128), F32)
    for r in range(ROUNDS):
        turned = quant[r].reshape(128, 128).T
        for i in range(3):
            st_send[3 * i + r : 3 * i + r + 1] = turned[i : i + 1]
        by_column = lf[r].reshape(128, 512).T
        picks = dot(by_column, own_parent, HIGHEST)
        picks = jnp.where(column == draft[r : r + 1], picks, 0.0)
        picks = jnp.sum(picks, axis=0, keepdims=True)
        st_send[9 + 2 * r : 10 + 2 * r] = picks[:, 0:128]
        st_send[10 + 2 * r : 11 + 2 * r] = picks[:, 128:256]

    def merge(ref):
        tile = ref[...]
        tops = tile[:, 0:3]
        top = jnp.max(tops, axis=0)
        shift = tops - top[None]
        factor = jnp.exp(shift)
        totals = tile[:, 3:6]
        total = jnp.sum(totals * factor, axis=0)
        spread = jnp.sum(factor * (tile[:, 6:9] + shift * totals), axis=0)
        picks = jnp.sum(tile[:, 9:16], axis=0)
        return jnp.concatenate([top, total, spread, picks], axis=0)

    mine = x * Y + y

    def sp_start(i, carry):
        j = lax.rem(mine + i, 16)
        send(
            st_send,
            st_plane.at[mine],
            sp_sem.at[0],
            sp_sem.at[1],
            dev(lax.div(j, Y), lax.rem(j, Y), z, c),
        )
        return carry

    lax.fori_loop(1, 16, sp_start, 0)
    st_plane[mine] = st_send[...]
    wait(st_plane.at[pl.ds(0, 15)], sp_sem.at[1])
    st_mid[...] = merge(st_plane)

    def sz_start(i, carry):
        send(
            st_mid, st_z.at[z], sz_sem.at[0], sz_sem.at[1], dev(x, y, zmate(i), c)
        )
        return carry

    lax.fori_loop(1, Z, sz_start, 0)
    st_z[z] = st_mid[...]
    wait(st_z.at[pl.ds(0, 15)], sz_sem.at[1])
    final = merge(st_z)
    st_own[...] = final
    send(st_own, st_sib, sb_sem.at[0], sb_sem.at[1], dev(x, y, z, sib))

    columns = jnp.concatenate([final, jnp.zeros((112, 128), F32)], axis=0).T
    other = pl.ds(pl.multiple_of(sib * COLS, COLS), COLS)
    ours = pl.ds(pl.multiple_of(c * COLS, COLS), COLS)
    for r in range(ROUNDS):
        top = columns[:, r : r + 1]
        inverse = 1.0 / columns[:, 3 + r : 4 + r]
        part = lf[r, :, :, other].reshape(128, COLS)
        psend[r] = (jnp.exp(part - top) * inverse).astype(BF16).reshape(8, 16, COLS)
    send(
        psend, prob.at[:, :, c], pr_sem.at[0], pr_sem.at[1], dev(x, y, z, sib)
    )
    for r in range(ROUNDS):
        top = columns[:, r : r + 1]
        inverse = 1.0 / columns[:, 3 + r : 4 + r]
        part = lf[r, :, :, ours].reshape(128, COLS)
        prob[r, :, c] = (jnp.exp(part - top) * inverse).astype(BF16).reshape(8, 16, COLS)

    wait(st_sib, sb_sem.at[1])
    even = jnp.where(c == 0, st_own[...], st_sib[...])
    odd = jnp.where(c == 0, st_sib[...], st_own[...])
    both = jnp.concatenate([even, odd], axis=1)
    log_total = jnp.log(both[3:6])
    log_norm = both[0:3] + log_total
    entropy = log_total - both[6:9] / both[3:6]
    stack = jnp.concatenate(
        [entropy, log_norm, jnp.zeros((2, 256), F32)], axis=0
    )
    place = iota((256, 256), 0)
    place = held(lax.rem(place, 128), lax.div(place, 128))
    in_order = dot(stack, (place == iota((256, 256), 1)).astype(F32), HIGHEST)
    of_parent = dot(stack, (place == parent_row).astype(F32), HIGHEST)
    picked = jnp.concatenate([even[9:15], odd[9:15]], axis=0)
    picked = jnp.concatenate(
        [
            jnp.concatenate(
                [
                    even[9 + 2 * r : 10 + 2 * r] + odd[9 + 2 * r : 10 + 2 * r],
                    even[10 + 2 * r : 11 + 2 * r] + odd[10 + 2 * r : 11 + 2 * r],
                ],
                axis=1,
            )
            for r in range(ROUNDS)
        ],
        axis=0,
    )
    log_draft = picked - of_parent[3:6]
    entropy_out[...] = in_order[0:3]
    margin_out[...] = log_draft + of_parent[0:3] - math.log(typical_alpha)

    tree = lax.div(iota((1, 256), 1), NODES)
    limits = []
    for r in range(ROUNDS):
        limit = jnp.zeros((1, 256), jnp.int32)
        for b in range(4):
            limit = jnp.where(tree == b, accepted[r, b], limit)
        limits.append(limit)
    limit = jnp.concatenate(limits, axis=0).astype(F32)
    survive = depth[0:3] < limit
    chosen = jnp.where(survive, log_draft, 0.0)
    in_tree = (lax.div(iota((256, 128), 0), NODES) == iota((256, 128), 1)).astype(F32)
    counted = dot(survive.astype(F32), in_tree, HIGHEST)
    score = dot(chosen, in_tree, HIGHEST)
    score_out[...] = score[:, 0:4] / counted[:, 0:4]

    wait(prob.at[:, :, 0], pr_sem.at[1])
    wait(psend, pr_sem.at[0])
    wait(st_own, sb_sem.at[0])
    wait(st_z.at[pl.ds(0, 15)], sz_sem.at[0])
    wait(st_plane.at[pl.ds(0, 15)], sp_sem.at[0])
    wait(lr, ls_sem.at[0])
    wait(xg.at[pl.ds(0, 3)], p2s_sem.at[0])
    wait(xg.at[0, pl.ds(0, 3)], p1s_sem.at[0])
    wait(xg.at[0, 0, pl.ds(0, 15)], zs_sem.at[0])
    wait(ss_recv.at[pl.ds(0, PLANE - 1)], ss_sem.at[0])
    wait(rs_recv.at[pl.ds(0, PLANE - 1)], rs_sem.at[0])
    swap_w.wait_send()


def body(partials, norm_gain, head_weight, draft_ids, tree_parents, accepted_lengths):
    vmem = pl.BlockSpec(memory_space=pltpu.VMEM)
    prob, entropy, margin, score = pl.pallas_call(
        kernel,
        out_shape=(
            jax.ShapeDtypeStruct((ROUNDS, 8, 2, 16, COLS), BF16),
            jax.ShapeDtypeStruct((ROUNDS, 256), F32),
            jax.ShapeDtypeStruct((ROUNDS, 256), F32),
            jax.ShapeDtypeStruct((ROUNDS, 4), F32),
        ),
        in_specs=[
            vmem,
            vmem,
            pl.BlockSpec(memory_space=pl.ANY),
            vmem,
            vmem,
            pl.BlockSpec(memory_space=pltpu.SMEM),
        ],
        out_specs=(vmem, vmem, vmem, vmem),
        scratch_shapes=[
            pltpu.VMEM((2, KHALF, COLS), BF16),
            pltpu.VMEM((PLANE, 16, 128), BF16),
            pltpu.VMEM((PLANE, 16, 128), BF16),
            pltpu.VMEM((8, 128), F32),
            pltpu.VMEM((PLANE, 8, 128), F32),
            pltpu.VMEM((X, Y, Z, 48, 128), BF16),
            pltpu.VMEM((Z, 48, 512), F32),
            pltpu.VMEM((8, 48, 512), F32),
            pltpu.VMEM((ROUNDS, 8, 16, 512), F32),
            pltpu.VMEM((ROUNDS, 8, 16, 128), F32),
            pltpu.VMEM((16, 128), F32),
            pltpu.VMEM((16, 16, 128), F32),
            pltpu.VMEM((16, 128), F32),
            pltpu.VMEM((Z, 16, 128), F32),
            pltpu.VMEM((16, 128), F32),
            pltpu.VMEM((16, 128), F32),
            pltpu.VMEM((ROUNDS, 8, 16, COLS), BF16),
            pltpu.SemaphoreType.DMA((3,)),
            pltpu.SemaphoreType.DMA((2,)),
            pltpu.SemaphoreType.DMA((2,)),
            pltpu.SemaphoreType.DMA((Z,)),
            pltpu.SemaphoreType.DMA((1,)),
            pltpu.SemaphoreType.DMA((Z,)),
            pltpu.SemaphoreType.DMA((1,)),
            pltpu.SemaphoreType.DMA((Z,)),
            pltpu.SemaphoreType.DMA((1,)),
            pltpu.SemaphoreType.DMA((4,)),
            pltpu.SemaphoreType.DMA((1,)),
            pltpu.SemaphoreType.DMA((2,)),
            pltpu.SemaphoreType.DMA((2,)),
            pltpu.SemaphoreType.DMA((2,)),
            pltpu.SemaphoreType.DMA((2,)),
        ],
        compiler_params=pltpu.CompilerParams(
            collective_id=0, has_side_effects=True, vmem_limit_bytes=40 * 2**20
        ),
        name="verify",
    )(
        partials,
        norm_gain.astype(F32).reshape(PLANE, 1, 128),
        head_weight,
        draft_ids,
        tree_parents.reshape(1, 256),
        accepted_lengths,
    )
    return prob.reshape(ROUNDS, 256, COLS), entropy, margin, score


def solution(mesh):
    placed = (P(None, "tensor", "vocab", None), P(), P(None, ("tensor", "vocab")), P(), P(), P())
    return jax.shard_map(
        body,
        mesh=mesh,
        in_specs=placed,
        out_specs=(P(None, None, ("tensor", "vocab")), P(), P(), P()),
        check_vma=False,
    )
```

```python
import math

import jax
import jax.numpy as jnp
from jax import lax
from jax.experimental import pallas as pl
from jax.experimental.pallas import tpu as pltpu
from jax.sharding import PartitionSpec as P

MESH = pl.DeviceIdType.MESH
HIGHEST = lax.Precision.HIGHEST
F32 = jnp.float32
BF16 = jnp.bfloat16

X = 4
Y = 4
Z = 16
PLANE = 32
KHALF = 2048
COLS = 256
ROUNDS = 3
NODES = 64
SEQ = (0, 1, -1, 5, -5, 3, -3, 4, -4, 7, -7, 8)
GIFTS = {1: (-1, 0), -1: (1, 1), 5: (-1, 2), -5: (1, 3)}
GIVEN = {2: 0, -2: 1, 6: 2, -6: 3}
GROUPS = ((0, 1, -1, 4), (2, 5, -5, -2), (-4, 3, -3, 8), (6, 7, -7, -6))
position = {o: n for n, o in enumerate(SEQ)}
position.update({2: 1, -2: 2, 6: 3, -6: 4})
LAG = 3
DONE = 2
HEADS = ((3, 0, 1), (5, 1, 2), (99, 2, 3), (99, 3, 4))
norm_eps = 1e-06
typical_alpha = 0.3


def dot(a, b, precision=None):
    return jnp.dot(a, b, precision=precision, preferred_element_type=F32)


def iota(shape, dim):
    return lax.broadcasted_iota(jnp.int32, shape, dim)


def kernel(
    partials,
    gain,
    weight,
    draft_in,
    parents_in,
    accepted_in,
    prob,
    small,
    pbuf,
    gbuf,
    draft,
    parents,
    accepted,
    wbuf,
    rs_send,
    rs_recv,
    ss_send,
    ss_recv,
    xg,
    lp,
    lr,
    lf,
    quant,
    st_send,
    st_plane,
    st_mid,
    st_z,
    st_own,
    st_sib,
    pk_send,
    pk_plane,
    pk_mid,
    pk_z,
    pk_own,
    pk_sib,
    psend,
    in_sem,
    w_sem,
    rs_sem,
    ss_sem,
    z_sem,
    zs_sem,
    p1_sem,
    p1s_sem,
    p2_sem,
    p2s_sem,
    p3_sem,
    p3s_sem,
    g_sem,
    gs_sem,
    l_sem,
    ls_sem,
    sp_sem,
    sz_sem,
    sb_sem,
    kp_sem,
    kz_sem,
    kb_sem,
    pr_sem,
):
    t = lax.axis_index("tensor")
    v = lax.axis_index("vocab")
    x = lax.rem(v, X)
    z = lax.div(v, X)
    y = lax.div(t, 2)
    c = lax.rem(t, 2)
    sib = 1 - c

    def dev(dx, dy, dz, dc):
        return (dy * 2 + dc, dz * X + dx)

    def wait(ref, sem):
        pltpu.make_async_copy(ref, ref, sem).wait()

    def send(src, dst, ssem, rsem, device):
        pltpu.make_async_remote_copy(
            src_ref=src,
            dst_ref=dst,
            send_sem=ssem,
            recv_sem=rsem,
            device_id=device,
            device_id_type=MESH,
        ).start()

    me = c * 16 + x * Y + y

    def plane_dev(j):
        return dev(lax.div(lax.rem(j, 16), Y), lax.rem(j, Y), z, lax.div(j, 16))

    def zmate(o):
        return lax.rem(z + o + Z, Z)

    barrier = pltpu.get_barrier_semaphore()

    def greet_plane(i, carry):
        j = lax.rem(me + i, PLANE)
        pl.semaphore_signal(barrier, inc=1, device_id=plane_dev(j), device_id_type=MESH)
        return carry

    def greet_z(i, carry):
        pl.semaphore_signal(
            barrier, inc=1, device_id=dev(x, y, zmate(i), c), device_id_type=MESH
        )
        return carry

    read_partials = pltpu.make_async_copy(partials.at[:, 0], pbuf, in_sem.at[0])
    read_partials.start()
    lax.fori_loop(1, Z, greet_z, 0)
    lax.fori_loop(1, PLANE, greet_plane, 0)
    reads = [
        pltpu.make_async_copy(src, dst, in_sem.at[1 + i])
        for i, (src, dst) in enumerate(
            ((gain, gbuf), (draft_in, draft), (parents_in, parents), (accepted_in, accepted))
        )
    ]
    for read in reads:
        read.start()

    own_w = pltpu.make_async_copy(
        weight.at[pl.ds(c * KHALF, KHALF)], wbuf.at[c], w_sem.at[0]
    )
    own_w.start()

    read_partials.wait()
    rows = [pbuf[r].astype(F32) for r in range(ROUNDS)]
    slab = jnp.concatenate(rows + [jnp.zeros_like(rows[0])], axis=0).astype(BF16)
    for j in range(PLANE):
        rs_send[j] = slab[:, j * 128 : (j + 1) * 128]

    common = iota((128, 128), 0) & iota((128, 128), 1)
    parity = jnp.zeros((128, 128), jnp.int32)
    for bit in range(7):
        parity = parity + (lax.shift_right_logical(common, bit) & 1)
    signs = (1 - 2 * (parity & 1)).astype(F32)

    for read in reads:
        read.wait()
    gains = gbuf[...].astype(F32).reshape(PLANE, 128)
    gain_row = jnp.sum(
        jnp.where(iota((PLANE, 128), 0) == me, gains, 0.0), axis=0, keepdims=True
    )

    pl.semaphore_wait(barrier, PLANE - 1 + Z - 1)

    def rs_start(i, carry):
        j = lax.rem(me + i, PLANE)
        send(rs_send.at[j], rs_recv.at[me], rs_sem.at[0], rs_sem.at[1], plane_dev(j))
        return carry

    lax.fori_loop(1, PLANE, rs_start, 0)
    rs_recv[me] = rs_send[me]

    swap_w = pltpu.make_async_remote_copy(
        src_ref=weight.at[pl.ds(sib * KHALF, KHALF)],
        dst_ref=wbuf.at[c],
        send_sem=w_sem.at[1],
        recv_sem=w_sem.at[2],
        device_id=dev(x, y, z, sib),
        device_id_type=MESH,
    )
    wait(rs_recv.at[pl.ds(0, PLANE - 1)], rs_sem.at[1])
    swap_w.start()

    pieces = []
    for dx in range(X):
        total = jnp.zeros((16, 128), F32)
        for dy in range(Y):
            for dc in range(2):
                total = total + rs_recv[dc * 16 + dx * Y + dy].astype(F32)
        pieces.append(total)
    hidden = jnp.concatenate(
        [pieces[dx][4 * r : 4 * r + 4] for r in range(ROUNDS) for dx in range(X)],
        axis=0,
    )
    square = jnp.concatenate([hidden * hidden, jnp.zeros((80, 128), F32)], axis=0)
    ss_send[...] = jnp.broadcast_to(
        jnp.sum(square.T, axis=0, keepdims=True), (8, 128)
    )

    def ss_start(i, carry):
        j = lax.rem(me + i, PLANE)
        send(ss_send, ss_recv.at[me], ss_sem.at[0], ss_sem.at[1], plane_dev(j))
        return carry

    lax.fori_loop(1, PLANE, ss_start, 0)
    ss_recv[me] = ss_send[...]
    wait(ss_recv.at[pl.ds(0, PLANE - 1)], ss_sem.at[1])
    sums = ss_recv[0]
    for j in range(1, PLANE):
        sums = sums + ss_recv[j]
    scale = lax.rsqrt(sums[0:1] * (1.0 / 4096.0) + norm_eps)
    scale = jnp.broadcast_to(scale, (128, 128)).T[0:48]
    normed = hidden * scale * gain_row
    rotated = dot(normed, signs, HIGHEST) * (1.0 / math.sqrt(128.0))
    def order_of(n):
        return lax.rem(n + c, 2)

    def place(o, dx, dy):
        order = order_of(position[o])
        return dy + order * (dx - dy), dx + order * (dy - dx)

    def plane_step(axis_is_y, i):
        return dev(
            lax.rem(x + i * (1 - axis_is_y), X), lax.rem(y + i * axis_is_y, Y), z, c
        )

    def chunk_at(o):
        line, spot = place(o, x, y)
        return xg.at[zmate(o), line, spot]

    mine = xg.at[z, place(0, x, y)[0], place(0, x, y)[1]]
    mine[...] = rotated.astype(BF16)

    def z_start(n):
        line, spot = place(SEQ[n], x, y)
        send(
            mine,
            xg.at[z, line, spot],
            zs_sem.at[0],
            z_sem.at[n],
            dev(x, y, zmate(-SEQ[n]), c),
        )

    def across(n):
        chunk = chunk_at(SEQ[n])

        def step(i, carry):
            send(chunk, chunk, p1s_sem.at[0], p1_sem.at[n], plane_step(order_of(n), i))
            return carry

        lax.fori_loop(1, 4, step, 0)

    def along(n):
        wait(xg.at[0, 0, pl.ds(0, 3)], p1_sem.at[n])
        line = xg.at[zmate(SEQ[n]), place(SEQ[n], x, y)[0]]
        for i in range(2):
            send(
                line,
                line,
                p2s_sem.at[0],
                p2_sem.at[n, i],
                plane_step(1 - order_of(n), 1 + 2 * i),
            )

    def onward(n):
        here = place(SEQ[n], x, y)[0]
        for i in range(2):
            wait(xg.at[0, 0], p2_sem.at[n, i])
            half = xg.at[zmate(SEQ[n]), lax.rem(here + 3 - 2 * i, 4), pl.ds(2 * i, 2)]
            send(
                half,
                half,
                p3s_sem.at[0],
                p3_sem.at[n],
                plane_step(1 - order_of(n), 1 + 2 * i),
            )

    def complete(n):
        wait(xg.at[0, 0], p3_sem.at[n])
        if SEQ[n] in GIFTS:
            step, index = GIFTS[SEQ[n]]
            whole = xg.at[zmate(SEQ[n])]
            send(whole, whole, gs_sem.at[0], g_sem.at[index], dev(x, y, zmate(step), c))

    same = lax.rem(z + c, 2)

    def own_plane(g, i):
        group = GROUPS[g]
        return zmate(group[3 * i] + same * (group[1 + i] - group[3 * i]))

    def sib_plane(g, i):
        group = GROUPS[g]
        return zmate(group[1 + i] + same * (group[3 * i] - group[1 + i]))

    def head(first, last):
        offsets = [o for g in range(first, last) for o in GROUPS[g]]
        for o in offsets:
            if o in GIVEN:
                wait(xg.at[0], g_sem.at[GIVEN[o]])
        chunks = []
        for o in offsets:
            pieces = []
            for dx in range(X):
                for dy in range(Y):
                    line, spot = place(o, dx, dy)
                    pieces.append(xg[zmate(o), line, spot])
            chunks.append(jnp.concatenate(pieces, axis=1))
        lhs = jnp.concatenate(chunks, axis=0)
        for cc in range(2):
            out = dot(lhs, wbuf[cc])
            for i, o in enumerate(offsets):
                lp[zmate(o), :, cc * COLS : (cc + 1) * COLS] = out[48 * i : 48 * i + 48]
        for g in range(first, last):
            for i in range(2):
                zs = sib_plane(g, i)
                send(
                    lp.at[zs],
                    lr.at[lax.div(zs, 2)],
                    ls_sem.at[0],
                    l_sem.at[g],
                    dev(x, y, z, sib),
                )

    def stats(g):
        wait(lr.at[pl.ds(0, 2)], l_sem.at[g])
        lane = iota((48, 128), 1)
        for i in range(2):
            zs = own_plane(g, i)
            zi = lax.div(zs, 2)
            full = lp[zs] + lr[zi]
            top = jnp.max(full, axis=1, keepdims=True)
            shifted = full - top
            weights = jnp.exp(shifted)
            total = jnp.sum(weights, axis=1, keepdims=True)
            spread = jnp.sum(weights * shifted, axis=1, keepdims=True)
            log_total = jnp.log(total)
            packed = jnp.where(lane == 0, top + log_total, log_total - spread / total)
            for r in range(ROUNDS):
                lf[r, zi] = full[16 * r : 16 * r + 16]
                quant[r, zi] = packed[16 * r : 16 * r + 16]

    count = len(SEQ)
    across(0)
    for n in range(1, count):
        z_start(n)
    for step in range(1, count + 2 * LAG + DONE):
        if step < count:
            wait(mine, z_sem.at[step])
            across(step)
        if LAG <= step < count + LAG:
            along(step - LAG)
        if 2 * LAG <= step < count + 2 * LAG:
            onward(step - 2 * LAG)
        if 2 * LAG + DONE <= step:
            complete(step - 2 * LAG - DONE)
        if step == count:
            own_w.wait()
            swap_w.wait_recv()
        for at, first, last in HEADS:
            if step == at + count:
                head(first, last)
    ready = 0
    for at, first, last in HEADS:
        if at + count >= count + 2 * LAG + DONE:
            head(first, last)
            for g in range(ready, last - 1):
                stats(g)
            ready = last - 1
    stats(len(GROUPS) - 1)

    chip = x * Y + y

    def plane_start(src, dst, sems):
        def step(i, carry):
            j = lax.rem(chip + i, 16)
            send(
                src,
                dst.at[chip],
                sems.at[0],
                sems.at[1],
                dev(lax.div(j, Y), lax.rem(j, Y), z, c),
            )
            return carry

        lax.fori_loop(1, 16, step, 0)
        dst[chip] = src[...]

    def line_start(src, dst, sems):
        def step(i, carry):
            send(src, dst.at[z], sems.at[0], sems.at[1], dev(x, y, zmate(i), c))
            return carry

        lax.fori_loop(1, Z, step, 0)
        dst[z] = src[...]

    def merge(ref):
        tile = ref[...]
        part_log, part_entropy = tile[:, 0:3], tile[:, 3:6]
        top = jnp.max(part_log, axis=0)
        share = jnp.exp(part_log - top[None])
        total = jnp.sum(share, axis=0)
        log_norm = top + jnp.log(total)
        spread = jnp.sum(share * (part_entropy + (log_norm[None] - part_log)), axis=0)
        return jnp.concatenate(
            [log_norm, spread / total, jnp.zeros((2, 128), F32)], axis=0
        )

    st_send[...] = jnp.zeros((8, 128), F32)
    for r in range(ROUNDS):
        turned = quant[r].reshape(128, 128).T
        for i in range(2):
            st_send[3 * i + r : 3 * i + r + 1] = turned[i : i + 1]
    plane_start(st_send, st_plane, sp_sem)

    def held(index, core):
        return (lax.div(index, 16) * 2 + core) * 16 + lax.rem(index, 16)

    parent_row = lax.div(iota((1, 256), 1), NODES) * NODES + parents[...]
    own_parent = (held(iota((128, 256), 0), c) == parent_row).astype(F32)
    column = iota((512, 256), 0)
    column = (
        ((y * 2 + lax.div(column, COLS)) * (X * Z) + v) * COLS + lax.rem(column, COLS)
    )
    pk_send[...] = jnp.zeros((8, 128), F32)
    for r in range(ROUNDS):
        by_column = lf[r].reshape(128, 512).T
        picks = dot(by_column, own_parent, HIGHEST)
        picks = jnp.where(column == draft[r : r + 1], picks, 0.0)
        picks = jnp.sum(picks, axis=0, keepdims=True)
        pk_send[2 * r : 2 * r + 1] = picks[:, 0:128]
        pk_send[2 * r + 1 : 2 * r + 2] = picks[:, 128:256]
    plane_start(pk_send, pk_plane, kp_sem)

    wait(st_plane.at[pl.ds(0, 15)], sp_sem.at[1])
    st_mid[...] = merge(st_plane)
    line_start(st_mid, st_z, sz_sem)
    wait(pk_plane.at[pl.ds(0, 15)], kp_sem.at[1])
    pk_mid[...] = jnp.sum(pk_plane[...], axis=0)
    line_start(pk_mid, pk_z, kz_sem)

    jump = (iota((256, 256), 0) == parent_row).astype(BF16)
    depth = jnp.broadcast_to(
        (lax.rem(iota((1, 256), 1), NODES) > 0).astype(F32), (8, 256)
    )
    for step in range(NODES.bit_length()):
        depth = depth + dot(depth.astype(BF16), jump)
        if step < NODES.bit_length() - 1:
            jump = dot(jump, jump).astype(BF16)

    wait(st_z.at[pl.ds(0, 15)], sz_sem.at[1])
    final = merge(st_z)
    st_own[...] = final
    send(st_own, st_sib, sb_sem.at[0], sb_sem.at[1], dev(x, y, z, sib))

    columns = jnp.concatenate([final, jnp.zeros((120, 128), F32)], axis=0).T
    other = pl.ds(pl.multiple_of(sib * COLS, COLS), COLS)
    ours = pl.ds(pl.multiple_of(c * COLS, COLS), COLS)
    for r in range(ROUNDS):
        part = lf[r, :, :, other].reshape(128, COLS) - columns[:, r : r + 1]
        psend[r] = jnp.exp(part).astype(BF16).reshape(8, 16, COLS)
    send(
        psend, prob.at[:, :, c], pr_sem.at[0], pr_sem.at[1], dev(x, y, z, sib)
    )
    for r in range(ROUNDS):
        part = lf[r, :, :, ours].reshape(128, COLS) - columns[:, r : r + 1]
        prob[r, :, c] = jnp.exp(part).astype(BF16).reshape(8, 16, COLS)

    wait(pk_z.at[pl.ds(0, 15)], kz_sem.at[1])
    pk_own[...] = jnp.sum(pk_z[...], axis=0)
    send(pk_own, pk_sib, kb_sem.at[0], kb_sem.at[1], dev(x, y, z, sib))

    wait(st_sib, sb_sem.at[1])
    even = jnp.where(c == 0, st_own[...], st_sib[...])
    odd = jnp.where(c == 0, st_sib[...], st_own[...])
    both = jnp.concatenate([even, odd], axis=1)
    spots = iota((256, 256), 0)
    spots = held(lax.rem(spots, 128), lax.div(spots, 128))
    in_order = dot(both, (spots == iota((256, 256), 1)).astype(F32), HIGHEST)
    of_parent = dot(both, (spots == parent_row).astype(F32), HIGHEST)

    tree = lax.div(iota((1, 256), 1), NODES)
    limits = []
    for r in range(ROUNDS):
        limit = jnp.zeros((1, 256), jnp.int32)
        for b in range(4):
            limit = jnp.where(tree == b, accepted[r : r + 1, b : b + 1], limit)
        limits.append(limit)
    limit = jnp.concatenate(limits, axis=0).astype(F32)
    survive = depth[0:3] < limit
    lane = iota((256, 128), 1)
    in_tree = (lax.div(iota((256, 128), 0), NODES) == lax.rem(lane, 4)).astype(F32)
    counted = dot(survive.astype(F32), in_tree, HIGHEST)

    wait(pk_sib, kb_sem.at[1])
    picks = jnp.where(c == 0, pk_own[...], pk_sib[...])
    picks = picks + jnp.where(c == 0, pk_sib[...], pk_own[...])
    picked = jnp.concatenate(
        [
            jnp.concatenate([picks[2 * r : 2 * r + 1], picks[2 * r + 1 : 2 * r + 2]], axis=1)
            for r in range(ROUNDS)
        ],
        axis=0,
    )
    log_draft = picked - of_parent[0:3]
    chosen = jnp.where(survive, log_draft, 0.0)
    score = dot(chosen, in_tree, HIGHEST) / counted
    small[0:3] = in_order[3:6]
    small[3:6] = log_draft + of_parent[3:6] - math.log(typical_alpha)
    small[8:11] = jnp.concatenate([score, score], axis=1)

    wait(prob.at[:, :, 0], pr_sem.at[1])
    wait(psend, pr_sem.at[0])
    wait(pk_own, kb_sem.at[0])
    wait(st_own, sb_sem.at[0])
    wait(pk_z.at[pl.ds(0, 15)], kz_sem.at[0])
    wait(st_z.at[pl.ds(0, 15)], sz_sem.at[0])
    wait(pk_plane.at[pl.ds(0, 15)], kp_sem.at[0])
    wait(st_plane.at[pl.ds(0, 15)], sp_sem.at[0])
    wait(lr, ls_sem.at[0])
    if GIFTS:
        wait(xg.at[pl.ds(0, len(GIFTS))], gs_sem.at[0])
    wait(xg.at[pl.ds(0, count), 0], p3s_sem.at[0])
    wait(xg.at[pl.ds(0, count), pl.ds(0, 2)], p2s_sem.at[0])
    wait(xg.at[pl.ds(0, count), 0, pl.ds(0, 3)], p1s_sem.at[0])
    wait(xg.at[pl.ds(0, count - 1), 0, 0], zs_sem.at[0])
    wait(ss_recv.at[pl.ds(0, PLANE - 1)], ss_sem.at[0])
    wait(rs_recv.at[pl.ds(0, PLANE - 1)], rs_sem.at[0])
    swap_w.wait_send()


def body(partials, norm_gain, head_weight, draft_ids, tree_parents, accepted_lengths):
    vmem = pl.BlockSpec(memory_space=pltpu.VMEM)
    hbm = pl.BlockSpec(memory_space=pltpu.HBM)
    tile = pltpu.VMEM((8, 128), F32)
    tiles = pltpu.VMEM((16, 8, 128), F32)
    one, two = pltpu.SemaphoreType.DMA((1,)), pltpu.SemaphoreType.DMA((2,))
    prob, small = pl.pallas_call(
        kernel,
        out_shape=(
            jax.ShapeDtypeStruct((ROUNDS, 8, 2, 16, COLS), BF16),
            jax.ShapeDtypeStruct((16, 256), F32),
        ),
        in_specs=[hbm] * 6,
        out_specs=(vmem, vmem),
        scratch_shapes=[
            pltpu.VMEM((ROUNDS, 4, 4096), BF16),
            pltpu.VMEM((4096,), BF16),
            pltpu.VMEM((ROUNDS, 256), jnp.int32),
            pltpu.VMEM((1, 256), jnp.int32),
            pltpu.VMEM((ROUNDS, 4), jnp.int32),
            pltpu.VMEM((2, KHALF, COLS), BF16),
            pltpu.VMEM((PLANE, 16, 128), BF16),
            pltpu.VMEM((PLANE, 16, 128), BF16),
            tile,
            pltpu.VMEM((PLANE, 8, 128), F32),
            pltpu.VMEM((Z, 4, 4, 48, 128), BF16),
            pltpu.VMEM((Z, 48, 512), F32),
            pltpu.VMEM((8, 48, 512), F32),
            pltpu.VMEM((ROUNDS, 8, 16, 512), F32),
            pltpu.VMEM((ROUNDS, 8, 16, 128), F32),
            tile,
            tiles,
            tile,
            tiles,
            tile,
            tile,
            tile,
            tiles,
            tile,
            tiles,
            tile,
            tile,
            pltpu.VMEM((ROUNDS, 8, 16, COLS), BF16),
            pltpu.SemaphoreType.DMA((5,)),
            pltpu.SemaphoreType.DMA((3,)),
            two,
            two,
            pltpu.SemaphoreType.DMA((Z,)),
            one,
            pltpu.SemaphoreType.DMA((Z,)),
            one,
            pltpu.SemaphoreType.DMA((Z, 2)),
            one,
            pltpu.SemaphoreType.DMA((Z,)),
            one,
            pltpu.SemaphoreType.DMA((4,)),
            one,
            pltpu.SemaphoreType.DMA((4,)),
            one,
            two,
            two,
            two,
            two,
            two,
            two,
            two,
        ],
        compiler_params=pltpu.CompilerParams(
            collective_id=0, has_side_effects=True, vmem_limit_bytes=40 * 2**20
        ),
        name="verify",
    )(
        *(
            pltpu.with_memory_space_constraint(a, pltpu.HBM)
            for a in (
                partials,
                norm_gain,
                head_weight,
                draft_ids,
                tree_parents.reshape(1, 256),
                accepted_lengths,
            )
        )
    )
    return (
        prob.reshape(ROUNDS, 256, COLS),
        small[0:3],
        small[3:6],
        small[8:11, 0:4],
    )


def solution(mesh):
    placed = (P(None, "tensor", "vocab", None), P(), P(None, ("tensor", "vocab")), P(), P(), P())
    return jax.shard_map(
        body,
        mesh=mesh,
        in_specs=placed,
        out_specs=(P(None, None, ("tensor", "vocab")), P(), P(), P()),
        check_vma=False,
    )
```

```python
import math

import jax
import jax.numpy as jnp
from jax import lax
from jax.experimental import pallas as pl
from jax.experimental.pallas import tpu as pltpu
from jax.sharding import PartitionSpec as P

MESH = pl.DeviceIdType.MESH
HIGHEST = lax.Precision.HIGHEST
F32 = jnp.float32
BF16 = jnp.bfloat16

X = 4
Y = 4
Z = 16
PLANE = 32
KHALF = 2048
COLS = 256
ROUNDS = 3
NODES = 64
SEQ = (0, 1, -1, 3, -3, 5, -5, 4, -4, 7, -7, 8)
GIFTS = {1: (-1, 0), -1: (1, 1), 5: (-1, 2), -5: (1, 3)}
GIVEN = {2: 0, -2: 1, 6: 2, -6: 3}
GROUPS = ((0, 1, -1, 4), (2, 3, -3, -2), (-4, 5, -5, 8), (6, 7, -7, -6))
position = {o: n for n, o in enumerate(SEQ)}
position.update({2: 1, -2: 2, 6: 5, -6: 6})
LAG = 3
DONE = 2
AHEAD = 11
DIRECT = 0
HEADS = ((3, 0, 1), (5, 1, 2), (99, 2, 3), (99, 3, 4))
norm_eps = 1e-06
typical_alpha = 0.3


def dot(a, b, precision=None):
    return jnp.dot(a, b, precision=precision, preferred_element_type=F32)


def iota(shape, dim):
    return lax.broadcasted_iota(jnp.int32, shape, dim)


def kernel(
    partials,
    gain,
    weight,
    draft_in,
    parents_in,
    accepted_in,
    prob,
    small,
    pbuf,
    gbuf,
    draft,
    parents,
    accepted,
    wbuf,
    rs_send,
    rs_recv,
    ss_send,
    ss_recv,
    xg,
    lp,
    lr,
    lf,
    quant,
    st_send,
    st_plane,
    st_mid,
    st_z,
    st_own,
    st_sib,
    pk_send,
    pk_plane,
    pk_mid,
    pk_z,
    psend,
    in_sem,
    w_sem,
    rs_sem,
    ss_sem,
    z_sem,
    zs_sem,
    p1_sem,
    p1s_sem,
    p2_sem,
    p2s_sem,
    p3_sem,
    p3s_sem,
    g_sem,
    gs_sem,
    ds_sem,
    l_sem,
    ls_sem,
    sp_sem,
    sz_sem,
    sb_sem,
    kp_sem,
    kz_sem,
    pr_sem,
    near_sem,
):
    t = lax.axis_index("tensor")
    v = lax.axis_index("vocab")
    x = lax.rem(v, X)
    z = lax.div(v, X)
    y = lax.div(t, 2)
    c = lax.rem(t, 2)
    sib = 1 - c

    def dev(dx, dy, dz, dc):
        return (dy * 2 + dc, dz * X + dx)

    def wait(ref, sem):
        pltpu.make_async_copy(ref, ref, sem).wait()

    def send(src, dst, ssem, rsem, device):
        pltpu.make_async_remote_copy(
            src_ref=src,
            dst_ref=dst,
            send_sem=ssem,
            recv_sem=rsem,
            device_id=device,
            device_id_type=MESH,
        ).start()

    me = c * 16 + x * Y + y

    def plane_dev(j):
        return dev(lax.div(lax.rem(j, 16), Y), lax.rem(j, Y), z, lax.div(j, 16))

    def zmate(o):
        return lax.rem(z + o + Z, Z)

    barrier = pltpu.get_barrier_semaphore()

    def greet_plane(i, carry):
        j = lax.rem(me + i, PLANE)
        pl.semaphore_signal(barrier, inc=1, device_id=plane_dev(j), device_id_type=MESH)
        return carry

    def greet_z(semaphore, distance):
        for o in (distance, -distance):
            pl.semaphore_signal(
                semaphore, inc=1, device_id=dev(x, y, zmate(o), c), device_id_type=MESH
            )

    read_partials = pltpu.make_async_copy(partials.at[:, 0], pbuf, in_sem.at[0])
    read_partials.start()
    greet_z(barrier, 1)
    lax.fori_loop(1, PLANE, greet_plane, 0)
    reads = [
        pltpu.make_async_copy(src, dst, in_sem.at[1 + i])
        for i, (src, dst) in enumerate(
            ((gain, gbuf), (draft_in, draft), (parents_in, parents), (accepted_in, accepted))
        )
    ]
    for read in reads:
        read.start()

    own_w = pltpu.make_async_copy(
        weight.at[pl.ds(c * KHALF, KHALF)], wbuf.at[c], w_sem.at[0]
    )
    own_w.start()

    read_partials.wait()
    rows = [pbuf[r].astype(F32) for r in range(ROUNDS)]
    slab = jnp.concatenate(rows + [jnp.zeros_like(rows[0])], axis=0).astype(BF16)
    for j in range(PLANE):
        rs_send[j] = slab[:, j * 128 : (j + 1) * 128]

    common = iota((128, 128), 0) & iota((128, 128), 1)
    parity = jnp.zeros((128, 128), jnp.int32)
    for bit in range(7):
        parity = parity + (lax.shift_right_logical(common, bit) & 1)
    signs = (1 - 2 * (parity & 1)).astype(F32)

    for read in reads:
        read.wait()
    gains = gbuf[...].astype(F32).reshape(PLANE, 128)
    gain_row = jnp.sum(
        jnp.where(iota((PLANE, 128), 0) == me, gains, 0.0), axis=0, keepdims=True
    )

    pl.semaphore_wait(barrier, PLANE - 1 + 2)
    greet_z(near_sem.at[0], 1)

    def rs_start(i, carry):
        j = lax.rem(me + i, PLANE)
        send(rs_send.at[j], rs_recv.at[me], rs_sem.at[0], rs_sem.at[1], plane_dev(j))
        return carry

    lax.fori_loop(1, PLANE, rs_start, 0)
    rs_recv[me] = rs_send[me]

    swap_w = pltpu.make_async_remote_copy(
        src_ref=weight.at[pl.ds(sib * KHALF, KHALF)],
        dst_ref=wbuf.at[c],
        send_sem=w_sem.at[1],
        recv_sem=w_sem.at[2],
        device_id=dev(x, y, z, sib),
        device_id_type=MESH,
    )
    pl.semaphore_wait(near_sem.at[0], 2)
    greet_z(near_sem.at[1], 2)
    wait(rs_recv.at[pl.ds(0, PLANE - 1)], rs_sem.at[1])
    swap_w.start()

    pieces = []
    for dx in range(X):
        total = jnp.zeros((16, 128), F32)
        for dy in range(Y):
            for dc in range(2):
                total = total + rs_recv[dc * 16 + dx * Y + dy].astype(F32)
        pieces.append(total)
    hidden = jnp.concatenate(
        [pieces[dx][4 * r : 4 * r + 4] for r in range(ROUNDS) for dx in range(X)],
        axis=0,
    )
    square = jnp.concatenate([hidden * hidden, jnp.zeros((80, 128), F32)], axis=0)
    ss_send[...] = jnp.broadcast_to(
        jnp.sum(square.T, axis=0, keepdims=True), (8, 128)
    )

    def ss_start(i, carry):
        j = lax.rem(me + i, PLANE)
        send(ss_send, ss_recv.at[me], ss_sem.at[0], ss_sem.at[1], plane_dev(j))
        return carry

    lax.fori_loop(1, PLANE, ss_start, 0)
    ss_recv[me] = ss_send[...]
    pl.semaphore_wait(near_sem.at[1], 2)
    greet_z(near_sem.at[2], 4)
    wait(ss_recv.at[pl.ds(0, PLANE - 1)], ss_sem.at[1])
    sums = ss_recv[0]
    for j in range(1, PLANE):
        sums = sums + ss_recv[j]
    scale = lax.rsqrt(sums[0:1] * (1.0 / 4096.0) + norm_eps)
    scale = jnp.broadcast_to(scale, (128, 128)).T[0:48]
    normed = hidden * scale * gain_row
    rotated = dot(normed, signs, HIGHEST) * (1.0 / math.sqrt(128.0))
    def order_of(n):
        return lax.rem(n + c, 2)

    def place(o, dx, dy):
        order = order_of(position[o])
        return dy + order * (dx - dy), dx + order * (dy - dx)

    def plane_step(axis_is_y, i):
        return dev(
            lax.rem(x + i * (1 - axis_is_y), X), lax.rem(y + i * axis_is_y, Y), z, c
        )

    def chunk_at(o):
        line, spot = place(o, x, y)
        return xg.at[zmate(o), line, spot]

    mine = xg.at[z, place(0, x, y)[0], place(0, x, y)[1]]
    mine[...] = rotated.astype(BF16)

    def z_start(n):
        line, spot = place(SEQ[n], x, y)
        send(
            mine,
            xg.at[z, line, spot],
            zs_sem.at[0],
            z_sem.at[n],
            dev(x, y, zmate(-SEQ[n]), c),
        )

    def across(n):
        chunk = chunk_at(SEQ[n])

        def step(i, carry):
            send(chunk, chunk, p1s_sem.at[0], p1_sem.at[n], plane_step(order_of(n), i))
            return carry

        lax.fori_loop(1, 4, step, 0)

    def along(n):
        wait(xg.at[0, 0, pl.ds(0, 3)], p1_sem.at[n])
        line = xg.at[zmate(SEQ[n]), place(SEQ[n], x, y)[0]]
        for i in range(2):
            send(
                line,
                line,
                p2s_sem.at[0],
                p2_sem.at[n, i],
                plane_step(1 - order_of(n), 1 + 2 * i),
            )

    def onward(n):
        here = place(SEQ[n], x, y)[0]
        for i in range(2):
            wait(xg.at[0, 0], p2_sem.at[n, i])
            half = xg.at[zmate(SEQ[n]), lax.rem(here + 3 - 2 * i, 4), pl.ds(2 * i, 2)]
            send(
                half,
                half,
                p3s_sem.at[0],
                p3_sem.at[n],
                plane_step(1 - order_of(n), 1 + 2 * i),
            )

    def spread(n):
        chunk = chunk_at(SEQ[n])

        def step(i, carry):
            j = lax.rem(x * Y + y + i, 16)
            target = dev(lax.div(j, Y), lax.rem(j, Y), z, c)
            send(chunk, chunk, ds_sem.at[0], p3_sem.at[n], target)
            return carry

        lax.fori_loop(1, 16, step, 0)

    def complete(n):
        wait(xg.at[0, 0] if n < stepped else xg.at[pl.ds(0, 15), 0, 0], p3_sem.at[n])
        if SEQ[n] in GIFTS:
            step, index = GIFTS[SEQ[n]]
            whole = xg.at[zmate(SEQ[n])]
            send(whole, whole, gs_sem.at[0], g_sem.at[index], dev(x, y, zmate(step), c))

    same = lax.rem(z + c, 2)

    def own_plane(g, i):
        group = GROUPS[g]
        return zmate(group[3 * i] + same * (group[1 + i] - group[3 * i]))

    def sib_plane(g, i):
        group = GROUPS[g]
        return zmate(group[1 + i] + same * (group[3 * i] - group[1 + i]))

    def head(first, last):
        offsets = [o for g in range(first, last) for o in GROUPS[g]]
        for o in offsets:
            if o in GIVEN:
                wait(xg.at[0], g_sem.at[GIVEN[o]])
        chunks = []
        for o in offsets:
            pieces = []
            for dx in range(X):
                for dy in range(Y):
                    line, spot = place(o, dx, dy)
                    pieces.append(xg[zmate(o), line, spot])
            chunks.append(jnp.concatenate(pieces, axis=1))
        lhs = jnp.concatenate(chunks, axis=0)
        for cc in range(2):
            out = dot(lhs, wbuf[cc])
            for i, o in enumerate(offsets):
                lp[zmate(o), :, cc * COLS : (cc + 1) * COLS] = out[48 * i : 48 * i + 48]
        for g in range(first, last):
            for i in range(2):
                zs = sib_plane(g, i)
                send(
                    lp.at[zs],
                    lr.at[lax.div(zs, 2)],
                    ls_sem.at[0],
                    l_sem.at[g],
                    dev(x, y, z, sib),
                )

    def stats(g):
        wait(lr.at[pl.ds(0, 2)], l_sem.at[g])
        lane = iota((48, 128), 1)
        for i in range(2):
            zs = own_plane(g, i)
            zi = lax.div(zs, 2)
            full = lp[zs] + lr[zi]
            top = jnp.max(full, axis=1, keepdims=True)
            shifted = full - top
            weights = jnp.exp(shifted)
            total = jnp.sum(weights, axis=1, keepdims=True)
            spread = jnp.sum(weights * shifted, axis=1, keepdims=True)
            log_total = jnp.log(total)
            packed = jnp.where(lane == 0, top + log_total, log_total - spread / total)
            for r in range(ROUNDS):
                lf[r, zi] = full[16 * r : 16 * r + 16]
                quant[r, zi] = packed[16 * r : 16 * r + 16]

    count = len(SEQ)
    stepped = count - DIRECT
    pl.semaphore_wait(near_sem.at[2], 2)
    for n in range(1, 1 + AHEAD):
        z_start(n)
    across(0)
    for step in range(1, count + 2 * LAG + DONE):
        if step + AHEAD < count:
            z_start(step + AHEAD)
        if step < count:
            wait(mine, z_sem.at[step])
            if step < stepped:
                across(step)
            else:
                spread(step)
        if LAG <= step < stepped + LAG:
            along(step - LAG)
        if 2 * LAG <= step < stepped + 2 * LAG:
            onward(step - 2 * LAG)
        if 2 * LAG + DONE <= step:
            complete(step - 2 * LAG - DONE)
        if step == count:
            own_w.wait()
            swap_w.wait_recv()
        for at, first, last in HEADS:
            if step == at + count:
                head(first, last)
    ready = 0
    for at, first, last in HEADS:
        if at + count >= count + 2 * LAG + DONE:
            head(first, last)
            for g in range(ready, last - 1):
                stats(g)
            ready = last - 1
    stats(len(GROUPS) - 1)

    chip = x * Y + y

    def plane_start(src, dst, sems):
        def step(i, carry):
            j = lax.rem(chip + i, 16)
            send(
                src,
                dst.at[chip],
                sems.at[0],
                sems.at[1],
                dev(lax.div(j, Y), lax.rem(j, Y), z, c),
            )
            return carry

        lax.fori_loop(1, 16, step, 0)
        dst[chip] = src[...]

    def line_start(src, dst, sems):
        def step(i, carry):
            send(src, dst.at[z], sems.at[0], sems.at[1], dev(x, y, zmate(i), c))
            return carry

        lax.fori_loop(1, Z, step, 0)
        dst[z] = src[...]

    def merge(ref):
        tile = ref[...]
        part_log, part_entropy = tile[:, 0:3], tile[:, 3:6]
        top = jnp.max(part_log, axis=0)
        share = jnp.exp(part_log - top[None])
        total = jnp.sum(share, axis=0)
        log_norm = top + jnp.log(total)
        spread = jnp.sum(share * (part_entropy + (log_norm[None] - part_log)), axis=0)
        return jnp.concatenate(
            [log_norm, spread / total, jnp.zeros((2, 128), F32)], axis=0
        )

    st_send[...] = jnp.zeros((8, 128), F32)
    for r in range(ROUNDS):
        turned = quant[r].reshape(128, 128).T
        for i in range(2):
            st_send[3 * i + r : 3 * i + r + 1] = turned[i : i + 1]
    plane_start(st_send, st_plane, sp_sem)

    def held(index, core):
        return (lax.div(index, 16) * 2 + core) * 16 + lax.rem(index, 16)

    parent_row = lax.div(iota((1, 256), 1), NODES) * NODES + parents[...]
    own_parent = (held(iota((128, 256), 0), c) == parent_row).astype(F32)
    column = iota((512, 256), 0)
    column = (
        ((y * 2 + lax.div(column, COLS)) * (X * Z) + v) * COLS + lax.rem(column, COLS)
    )
    pk_send[...] = jnp.zeros((8, 128), F32)
    for r in range(ROUNDS):
        by_column = lf[r].reshape(128, 512).T
        picks = dot(by_column, own_parent, HIGHEST)
        picks = jnp.where(column == draft[r : r + 1], picks, 0.0)
        picks = jnp.sum(picks, axis=0, keepdims=True)
        pk_send[2 * r : 2 * r + 1] = picks[:, 0:128]
        pk_send[2 * r + 1 : 2 * r + 2] = picks[:, 128:256]

    def pk_start(i, carry):
        j = lax.rem(me + i, PLANE)
        send(pk_send, pk_plane.at[me], kp_sem.at[0], kp_sem.at[1], plane_dev(j))
        return carry

    lax.fori_loop(1, PLANE, pk_start, 0)
    pk_plane[me] = pk_send[...]

    wait(st_plane.at[pl.ds(0, 15)], sp_sem.at[1])
    st_mid[...] = merge(st_plane)
    line_start(st_mid, st_z, sz_sem)
    wait(pk_plane.at[pl.ds(0, PLANE - 1)], kp_sem.at[1])
    pk_mid[...] = jnp.sum(pk_plane[...], axis=0)
    line_start(pk_mid, pk_z, kz_sem)

    jump = (iota((256, 256), 0) == parent_row).astype(BF16)
    depth = jnp.broadcast_to(
        (lax.rem(iota((1, 256), 1), NODES) > 0).astype(F32), (8, 256)
    )
    for step in range(NODES.bit_length()):
        depth = depth + dot(depth.astype(BF16), jump)
        if step < NODES.bit_length() - 1:
            jump = dot(jump, jump).astype(BF16)

    wait(st_z.at[pl.ds(0, 15)], sz_sem.at[1])
    final = merge(st_z)
    st_own[...] = final
    send(st_own, st_sib, sb_sem.at[0], sb_sem.at[1], dev(x, y, z, sib))

    columns = jnp.concatenate([final, jnp.zeros((120, 128), F32)], axis=0).T
    other = pl.ds(pl.multiple_of(sib * COLS, COLS), COLS)
    ours = pl.ds(pl.multiple_of(c * COLS, COLS), COLS)
    for r in range(ROUNDS):
        part = lf[r, :, :, other].reshape(128, COLS) - columns[:, r : r + 1]
        psend[r] = jnp.exp(part).astype(BF16).reshape(8, 16, COLS)
        send(
            psend.at[r], prob.at[r, :, c], pr_sem.at[0], pr_sem.at[1], dev(x, y, z, sib)
        )
    for r in range(ROUNDS):
        part = lf[r, :, :, ours].reshape(128, COLS) - columns[:, r : r + 1]
        prob[r, :, c] = jnp.exp(part).astype(BF16).reshape(8, 16, COLS)

    wait(st_sib, sb_sem.at[1])
    even = jnp.where(c == 0, st_own[...], st_sib[...])
    odd = jnp.where(c == 0, st_sib[...], st_own[...])
    both = jnp.concatenate([even, odd], axis=1)
    spots = iota((256, 256), 0)
    spots = held(lax.rem(spots, 128), lax.div(spots, 128))
    in_order = dot(both, (spots == iota((256, 256), 1)).astype(F32), HIGHEST)
    of_parent = dot(both, (spots == parent_row).astype(F32), HIGHEST)

    tree = lax.div(iota((1, 256), 1), NODES)
    limits = []
    for r in range(ROUNDS):
        limit = jnp.zeros((1, 256), jnp.int32)
        for b in range(4):
            limit = jnp.where(tree == b, accepted[r : r + 1, b : b + 1], limit)
        limits.append(limit)
    limit = jnp.concatenate(limits, axis=0).astype(F32)
    survive = depth[0:3] < limit
    lane = iota((256, 128), 1)
    in_tree = (lax.div(iota((256, 128), 0), NODES) == lax.rem(lane, 4)).astype(F32)
    counted = dot(survive.astype(F32), in_tree, HIGHEST)

    wait(pk_z.at[pl.ds(0, 15)], kz_sem.at[1])
    picks = jnp.sum(pk_z[...], axis=0)
    picked = jnp.concatenate(
        [
            jnp.concatenate([picks[2 * r : 2 * r + 1], picks[2 * r + 1 : 2 * r + 2]], axis=1)
            for r in range(ROUNDS)
        ],
        axis=0,
    )
    log_draft = picked - of_parent[0:3]
    chosen = jnp.where(survive, log_draft, 0.0)
    score = dot(chosen, in_tree, HIGHEST) / counted
    small[0:3] = in_order[3:6]
    small[3:6] = log_draft + of_parent[3:6] - math.log(typical_alpha)
    small[8:11] = jnp.concatenate([score, score], axis=1)

    wait(prob.at[:, :, 0], pr_sem.at[1])
    wait(psend, pr_sem.at[0])
    wait(st_own, sb_sem.at[0])
    wait(pk_z.at[pl.ds(0, 15)], kz_sem.at[0])
    wait(st_z.at[pl.ds(0, 15)], sz_sem.at[0])
    wait(pk_plane.at[pl.ds(0, PLANE - 1)], kp_sem.at[0])
    wait(st_plane.at[pl.ds(0, 15)], sp_sem.at[0])
    wait(lr, ls_sem.at[0])
    if GIFTS:
        wait(xg.at[pl.ds(0, len(GIFTS))], gs_sem.at[0])
    if DIRECT:
        wait(xg.at[pl.ds(0, 15), 0, pl.ds(0, DIRECT)], ds_sem.at[0])
    wait(xg.at[pl.ds(0, stepped), 0], p3s_sem.at[0])
    wait(xg.at[pl.ds(0, stepped), pl.ds(0, 2)], p2s_sem.at[0])
    wait(xg.at[pl.ds(0, stepped), 0, pl.ds(0, 3)], p1s_sem.at[0])
    wait(xg.at[pl.ds(0, count - 1), 0, 0], zs_sem.at[0])
    wait(ss_recv.at[pl.ds(0, PLANE - 1)], ss_sem.at[0])
    wait(rs_recv.at[pl.ds(0, PLANE - 1)], rs_sem.at[0])
    swap_w.wait_send()


def body(partials, norm_gain, head_weight, draft_ids, tree_parents, accepted_lengths):
    vmem = pl.BlockSpec(memory_space=pltpu.VMEM)
    hbm = pl.BlockSpec(memory_space=pltpu.HBM)
    tile = pltpu.VMEM((8, 128), F32)
    tiles = pltpu.VMEM((16, 8, 128), F32)
    one, two = pltpu.SemaphoreType.DMA((1,)), pltpu.SemaphoreType.DMA((2,))
    prob, small = pl.pallas_call(
        kernel,
        out_shape=(
            jax.ShapeDtypeStruct((ROUNDS, 8, 2, 16, COLS), BF16),
            jax.ShapeDtypeStruct((16, 256), F32),
        ),
        in_specs=[hbm] * 6,
        out_specs=(vmem, vmem),
        scratch_shapes=[
            pltpu.VMEM((ROUNDS, 4, 4096), BF16),
            pltpu.VMEM((4096,), BF16),
            pltpu.VMEM((ROUNDS, 256), jnp.int32),
            pltpu.VMEM((1, 256), jnp.int32),
            pltpu.VMEM((ROUNDS, 4), jnp.int32),
            pltpu.VMEM((2, KHALF, COLS), BF16),
            pltpu.VMEM((PLANE, 16, 128), BF16),
            pltpu.VMEM((PLANE, 16, 128), BF16),
            tile,
            pltpu.VMEM((PLANE, 8, 128), F32),
            pltpu.VMEM((Z, 4, 4, 48, 128), BF16),
            pltpu.VMEM((Z, 48, 512), F32),
            pltpu.VMEM((8, 48, 512), F32),
            pltpu.VMEM((ROUNDS, 8, 16, 512), F32),
            pltpu.VMEM((ROUNDS, 8, 16, 128), F32),
            tile,
            tiles,
            tile,
            tiles,
            tile,
            tile,
            tile,
            pltpu.VMEM((PLANE, 8, 128), F32),
            tile,
            tiles,
            pltpu.VMEM((ROUNDS, 8, 16, COLS), BF16),
            pltpu.SemaphoreType.DMA((5,)),
            pltpu.SemaphoreType.DMA((3,)),
            two,
            two,
            pltpu.SemaphoreType.DMA((Z,)),
            one,
            pltpu.SemaphoreType.DMA((Z,)),
            one,
            pltpu.SemaphoreType.DMA((Z, 2)),
            one,
            pltpu.SemaphoreType.DMA((Z,)),
            one,
            pltpu.SemaphoreType.DMA((4,)),
            one,
            one,
            pltpu.SemaphoreType.DMA((4,)),
            one,
            two,
            two,
            two,
            two,
            two,
            two,
            pltpu.SemaphoreType.REGULAR((3,)),
        ],
        compiler_params=pltpu.CompilerParams(
            collective_id=0, has_side_effects=True, vmem_limit_bytes=40 * 2**20
        ),
        name="verify",
    )(
        *(
            pltpu.with_memory_space_constraint(a, pltpu.HBM)
            for a in (
                partials,
                norm_gain,
                head_weight,
                draft_ids,
                tree_parents.reshape(1, 256),
                accepted_lengths,
            )
        )
    )
    return (
        prob.reshape(ROUNDS, 256, COLS),
        small[0:3],
        small[3:6],
        small[8:11, 0:4],
    )


def solution(mesh):
    placed = (P(None, "tensor", "vocab", None), P(), P(None, ("tensor", "vocab")), P(), P(), P())
    return jax.shard_map(
        body,
        mesh=mesh,
        in_specs=placed,
        out_specs=(P(None, None, ("tensor", "vocab")), P(), P(), P()),
        check_vma=False,
    )
```

```python
import math

import jax
import jax.numpy as jnp
from jax import lax
from jax.experimental import pallas as pl
from jax.experimental.pallas import tpu as pltpu
from jax.sharding import PartitionSpec as P

MESH = pl.DeviceIdType.MESH
HIGHEST = lax.Precision.HIGHEST
F32 = jnp.float32
BF16 = jnp.bfloat16

X = 4
Y = 4
Z = 16
PLANE = 32
KHALF = 2048
COLS = 256
ROUNDS = 3
NODES = 64
SEQ = (0, 1, -1, 3, -3, 5, -5, 4, -4, 7, -7, 8)
GIFTS = {1: (-1, 0), -1: (1, 1), 5: (-1, 2), -5: (1, 3)}
GIVEN = {2: 0, -2: 1, 6: 2, -6: 3}
GROUPS = ((0, 1, -1, 2), (-2, 3, -3, 4), (-4, 5, -5, 6), (8, 7, -7, -6))
position = {o: n for n, o in enumerate(SEQ)}
position.update({2: 1, -2: 2, 6: 5, -6: 6})
LAG = 3
DONE = 3
AHEAD = 11
DIRECT = 0
HEADS = ((4, 0, 1), (6, 1, 2), (99, 2, 3), (99, 3, 4))
norm_eps = 1e-06
typical_alpha = 0.3


def dot(a, b, precision=None):
    return jnp.dot(a, b, precision=precision, preferred_element_type=F32)


def iota(shape, dim):
    return lax.broadcasted_iota(jnp.int32, shape, dim)


def kernel(
    partials,
    gain,
    weight,
    draft_in,
    parents_in,
    accepted_in,
    prob,
    small,
    pbuf,
    gbuf,
    draft,
    parents,
    accepted,
    wbuf,
    rs_send,
    rs_recv,
    ss_send,
    ss_recv,
    xg,
    lp,
    lr,
    lf,
    quant,
    st_send,
    st_plane,
    st_mid,
    st_z,
    st_own,
    st_sib,
    pk_send,
    pk_plane,
    pk_mid,
    pk_z,
    psend,
    in_sem,
    w_sem,
    rs_sem,
    ss_sem,
    z_sem,
    zs_sem,
    p1_sem,
    p1s_sem,
    p2_sem,
    p2s_sem,
    p3_sem,
    p3s_sem,
    g_sem,
    gs_sem,
    ds_sem,
    l_sem,
    ls_sem,
    sp_sem,
    sz_sem,
    sb_sem,
    kp_sem,
    kz_sem,
    pr_sem,
    near_sem,
):
    t = lax.axis_index("tensor")
    v = lax.axis_index("vocab")
    x = lax.rem(v, X)
    z = lax.div(v, X)
    y = lax.div(t, 2)
    c = lax.rem(t, 2)
    sib = 1 - c

    def dev(dx, dy, dz, dc):
        return (dy * 2 + dc, dz * X + dx)

    def wait(ref, sem):
        pltpu.make_async_copy(ref, ref, sem).wait()

    def send(src, dst, ssem, rsem, device):
        pltpu.make_async_remote_copy(
            src_ref=src,
            dst_ref=dst,
            send_sem=ssem,
            recv_sem=rsem,
            device_id=device,
            device_id_type=MESH,
        ).start()

    me = c * 16 + x * Y + y

    def plane_dev(j):
        return dev(lax.div(lax.rem(j, 16), Y), lax.rem(j, Y), z, lax.div(j, 16))

    def zmate(o):
        return lax.rem(z + o + Z, Z)

    barrier = pltpu.get_barrier_semaphore()

    def greet_plane(i, carry):
        j = lax.rem(me + i, PLANE)
        pl.semaphore_signal(barrier, inc=1, device_id=plane_dev(j), device_id_type=MESH)
        return carry

    def greet_z(semaphore, distance):
        for o in (distance, -distance):
            pl.semaphore_signal(
                semaphore, inc=1, device_id=dev(x, y, zmate(o), c), device_id_type=MESH
            )

    read_partials = pltpu.make_async_copy(partials.at[:, 0], pbuf, in_sem.at[0])
    read_partials.start()
    greet_z(barrier, 1)
    lax.fori_loop(1, PLANE, greet_plane, 0)
    reads = [
        pltpu.make_async_copy(src, dst, in_sem.at[1 + i])
        for i, (src, dst) in enumerate(
            ((gain, gbuf), (draft_in, draft), (parents_in, parents), (accepted_in, accepted))
        )
    ]
    for read in reads:
        read.start()

    own_w = pltpu.make_async_copy(
        weight.at[pl.ds(c * KHALF, KHALF)], wbuf.at[c], w_sem.at[0]
    )
    own_w.start()

    read_partials.wait()
    rows = [pbuf[r].astype(F32) for r in range(ROUNDS)]
    slab = jnp.concatenate(rows + [jnp.zeros_like(rows[0])], axis=0).astype(BF16)
    for j in range(PLANE):
        rs_send[j] = slab[:, j * 128 : (j + 1) * 128]

    common = iota((128, 128), 0) & iota((128, 128), 1)
    parity = jnp.zeros((128, 128), jnp.int32)
    for bit in range(7):
        parity = parity + (lax.shift_right_logical(common, bit) & 1)
    signs = (1 - 2 * (parity & 1)).astype(F32)

    for read in reads:
        read.wait()
    gains = gbuf[...].astype(F32).reshape(PLANE, 128)
    gain_row = jnp.sum(
        jnp.where(iota((PLANE, 128), 0) == me, gains, 0.0), axis=0, keepdims=True
    )

    pl.semaphore_wait(barrier, PLANE - 1 + 2)
    greet_z(near_sem.at[0], 1)

    def rs_start(i, carry):
        j = lax.rem(me + i, PLANE)
        send(rs_send.at[j], rs_recv.at[me], rs_sem.at[0], rs_sem.at[1], plane_dev(j))
        return carry

    lax.fori_loop(1, PLANE, rs_start, 0)
    rs_recv[me] = rs_send[me]

    swap_w = pltpu.make_async_remote_copy(
        src_ref=weight.at[pl.ds(sib * KHALF, KHALF)],
        dst_ref=wbuf.at[c],
        send_sem=w_sem.at[1],
        recv_sem=w_sem.at[2],
        device_id=dev(x, y, z, sib),
        device_id_type=MESH,
    )
    pl.semaphore_wait(near_sem.at[0], 2)
    greet_z(near_sem.at[1], 2)
    wait(rs_recv.at[pl.ds(0, PLANE - 1)], rs_sem.at[1])
    swap_w.start()

    pieces = []
    for dx in range(X):
        total = jnp.zeros((16, 128), F32)
        for dy in range(Y):
            for dc in range(2):
                total = total + rs_recv[dc * 16 + dx * Y + dy].astype(F32)
        pieces.append(total)
    hidden = jnp.concatenate(
        [pieces[dx][4 * r : 4 * r + 4] for r in range(ROUNDS) for dx in range(X)],
        axis=0,
    )
    square = jnp.concatenate([hidden * hidden, jnp.zeros((80, 128), F32)], axis=0)
    ss_send[...] = jnp.broadcast_to(
        jnp.sum(square.T, axis=0, keepdims=True), (8, 128)
    )

    def ss_start(i, carry):
        j = lax.rem(me + i, PLANE)
        send(ss_send, ss_recv.at[me], ss_sem.at[0], ss_sem.at[1], plane_dev(j))
        return carry

    lax.fori_loop(1, PLANE, ss_start, 0)
    ss_recv[me] = ss_send[...]
    pl.semaphore_wait(near_sem.at[1], 2)
    greet_z(near_sem.at[2], 4)
    wait(ss_recv.at[pl.ds(0, PLANE - 1)], ss_sem.at[1])
    sums = ss_recv[0]
    for j in range(1, PLANE):
        sums = sums + ss_recv[j]
    scale = lax.rsqrt(sums[0:1] * (1.0 / 4096.0) + norm_eps)
    scale = jnp.broadcast_to(scale, (128, 128)).T[0:48]
    normed = hidden * scale * gain_row
    rotated = dot(normed, signs, HIGHEST) * (1.0 / math.sqrt(128.0))
    def order_of(n):
        return lax.rem(n + c, 2)

    def place(o, dx, dy):
        order = order_of(position[o])
        return dy + order * (dx - dy), dx + order * (dy - dx)

    def plane_step(axis_is_y, i):
        return dev(
            lax.rem(x + i * (1 - axis_is_y), X), lax.rem(y + i * axis_is_y, Y), z, c
        )

    def chunk_at(o):
        line, spot = place(o, x, y)
        return xg.at[zmate(o), line, spot]

    mine = xg.at[z, place(0, x, y)[0], place(0, x, y)[1]]
    mine[...] = rotated.astype(BF16)

    def z_start(n):
        line, spot = place(SEQ[n], x, y)
        send(
            mine,
            xg.at[z, line, spot],
            zs_sem.at[0],
            z_sem.at[n],
            dev(x, y, zmate(-SEQ[n]), c),
        )

    def across(n):
        chunk = chunk_at(SEQ[n])

        def step(i, carry):
            send(chunk, chunk, p1s_sem.at[0], p1_sem.at[n], plane_step(order_of(n), i))
            return carry

        lax.fori_loop(1, 4, step, 0)

    def along(n):
        wait(xg.at[0, 0, pl.ds(0, 3)], p1_sem.at[n])
        line = xg.at[zmate(SEQ[n]), place(SEQ[n], x, y)[0]]
        for i in range(2):
            send(
                line,
                line,
                p2s_sem.at[0],
                p2_sem.at[n, i],
                plane_step(1 - order_of(n), 1 + 2 * i),
            )

    def onward(n):
        here = place(SEQ[n], x, y)[0]
        for i in range(2):
            wait(xg.at[0, 0], p2_sem.at[n, i])
            half = xg.at[zmate(SEQ[n]), lax.rem(here + 3 - 2 * i, 4), pl.ds(2 * i, 2)]
            send(
                half,
                half,
                p3s_sem.at[0],
                p3_sem.at[n],
                plane_step(1 - order_of(n), 1 + 2 * i),
            )

    def spread(n):
        chunk = chunk_at(SEQ[n])

        def step(i, carry):
            j = lax.rem(x * Y + y + i, 16)
            target = dev(lax.div(j, Y), lax.rem(j, Y), z, c)
            send(chunk, chunk, ds_sem.at[0], p3_sem.at[n], target)
            return carry

        lax.fori_loop(1, 16, step, 0)

    def complete(n):
        wait(xg.at[0, 0] if n < stepped else xg.at[pl.ds(0, 15), 0, 0], p3_sem.at[n])
        if SEQ[n] in GIFTS:
            step, index = GIFTS[SEQ[n]]
            whole = xg.at[zmate(SEQ[n])]
            send(whole, whole, gs_sem.at[0], g_sem.at[index], dev(x, y, zmate(step), c))

    same = lax.rem(z + c, 2)

    def own_plane(g, i):
        group = GROUPS[g]
        return zmate(group[3 * i] + same * (group[1 + i] - group[3 * i]))

    def sib_plane(g, i):
        group = GROUPS[g]
        return zmate(group[1 + i] + same * (group[3 * i] - group[1 + i]))

    def head(first, last):
        offsets = [o for g in range(first, last) for o in GROUPS[g]]
        for o in offsets:
            if o in GIVEN:
                wait(xg.at[0], g_sem.at[GIVEN[o]])
        chunks = []
        for o in offsets:
            pieces = []
            for dx in range(X):
                for dy in range(Y):
                    line, spot = place(o, dx, dy)
                    pieces.append(xg[zmate(o), line, spot])
            chunks.append(jnp.concatenate(pieces, axis=1))
        lhs = jnp.concatenate(chunks, axis=0)
        for cc in range(2):
            out = dot(lhs, wbuf[cc])
            for i, o in enumerate(offsets):
                lp[zmate(o), :, cc * COLS : (cc + 1) * COLS] = out[48 * i : 48 * i + 48]
        for g in range(first, last):
            for i in range(2):
                zs = sib_plane(g, i)
                send(
                    lp.at[zs],
                    lr.at[lax.div(zs, 2)],
                    ls_sem.at[0],
                    l_sem.at[g],
                    dev(x, y, z, sib),
                )

    def stats(g):
        wait(lr.at[pl.ds(0, 2)], l_sem.at[g])
        lane = iota((48, 128), 1)
        for i in range(2):
            zs = own_plane(g, i)
            zi = lax.div(zs, 2)
            full = lp[zs] + lr[zi]
            top = jnp.max(full, axis=1, keepdims=True)
            shifted = full - top
            weights = jnp.exp(shifted)
            total = jnp.sum(weights, axis=1, keepdims=True)
            spread = jnp.sum(weights * shifted, axis=1, keepdims=True)
            log_total = jnp.log(total)
            packed = jnp.where(lane == 0, top + log_total, log_total - spread / total)
            for r in range(ROUNDS):
                lf[r, zi] = full[16 * r : 16 * r + 16]
                quant[r, zi] = packed[16 * r : 16 * r + 16]

    count = len(SEQ)
    stepped = count - DIRECT
    pl.semaphore_wait(near_sem.at[2], 2)
    for n in range(1, 1 + AHEAD):
        z_start(n)
    across(0)
    for step in range(1, count + 2 * LAG + DONE):
        if step + AHEAD < count:
            z_start(step + AHEAD)
        if step < count:
            wait(mine, z_sem.at[step])
            if step < stepped:
                across(step)
            else:
                spread(step)
        if LAG <= step < stepped + LAG:
            along(step - LAG)
        if 2 * LAG <= step < stepped + 2 * LAG:
            onward(step - 2 * LAG)
        if 2 * LAG + DONE <= step:
            complete(step - 2 * LAG - DONE)
        if step == count:
            own_w.wait()
            swap_w.wait_recv()
        for at, first, last in HEADS:
            if step == at + count:
                head(first, last)
    ready = 0
    for at, first, last in HEADS:
        if at + count >= count + 2 * LAG + DONE:
            head(first, last)
            for g in range(ready, last - 1):
                stats(g)
            ready = last - 1
    stats(len(GROUPS) - 1)

    chip = x * Y + y

    def plane_start(src, dst, sems):
        def step(i, carry):
            j = lax.rem(chip + i, 16)
            send(
                src,
                dst.at[chip],
                sems.at[0],
                sems.at[1],
                dev(lax.div(j, Y), lax.rem(j, Y), z, c),
            )
            return carry

        lax.fori_loop(1, 16, step, 0)
        dst[chip] = src[...]

    def line_start(src, dst, sems):
        def step(i, carry):
            send(src, dst.at[z], sems.at[0], sems.at[1], dev(x, y, zmate(i), c))
            return carry

        lax.fori_loop(1, Z, step, 0)
        dst[z] = src[...]

    def merge(ref):
        tile = ref[...]
        part_log, part_entropy = tile[:, 0:3], tile[:, 3:6]
        top = jnp.max(part_log, axis=0)
        share = jnp.exp(part_log - top[None])
        total = jnp.sum(share, axis=0)
        log_norm = top + jnp.log(total)
        spread = jnp.sum(share * (part_entropy + (log_norm[None] - part_log)), axis=0)
        return jnp.concatenate(
            [log_norm, spread / total, jnp.zeros((2, 128), F32)], axis=0
        )

    st_send[...] = jnp.zeros((8, 128), F32)
    for r in range(ROUNDS):
        turned = quant[r].reshape(128, 128).T
        for i in range(2):
            st_send[3 * i + r : 3 * i + r + 1] = turned[i : i + 1]
    plane_start(st_send, st_plane, sp_sem)

    def held(index, core):
        return (lax.div(index, 16) * 2 + core) * 16 + lax.rem(index, 16)

    parent_row = lax.div(iota((1, 256), 1), NODES) * NODES + parents[...]
    own_parent = (held(iota((128, 256), 0), c) == parent_row).astype(F32)
    column = iota((512, 256), 0)
    column = (
        ((y * 2 + lax.div(column, COLS)) * (X * Z) + v) * COLS + lax.rem(column, COLS)
    )
    pk_send[...] = jnp.zeros((8, 128), F32)
    for r in range(ROUNDS):
        by_column = lf[r].reshape(128, 512).T
        picks = dot(by_column, own_parent, HIGHEST)
        picks = jnp.where(column == draft[r : r + 1], picks, 0.0)
        picks = jnp.sum(picks, axis=0, keepdims=True)
        pk_send[2 * r : 2 * r + 1] = picks[:, 0:128]
        pk_send[2 * r + 1 : 2 * r + 2] = picks[:, 128:256]

    def pk_start(i, carry):
        j = lax.rem(me + i, PLANE)
        send(pk_send, pk_plane.at[me], kp_sem.at[0], kp_sem.at[1], plane_dev(j))
        return carry

    lax.fori_loop(1, PLANE, pk_start, 0)
    pk_plane[me] = pk_send[...]

    wait(st_plane.at[pl.ds(0, 15)], sp_sem.at[1])
    st_mid[...] = merge(st_plane)
    line_start(st_mid, st_z, sz_sem)
    wait(pk_plane.at[pl.ds(0, PLANE - 1)], kp_sem.at[1])
    pk_mid[...] = jnp.sum(pk_plane[...], axis=0)
    line_start(pk_mid, pk_z, kz_sem)

    jump = (iota((256, 256), 0) == parent_row).astype(BF16)
    depth = jnp.broadcast_to(
        (lax.rem(iota((1, 256), 1), NODES) > 0).astype(F32), (8, 256)
    )
    for step in range(NODES.bit_length()):
        depth = depth + dot(depth.astype(BF16), jump)
        if step < NODES.bit_length() - 1:
            jump = dot(jump, jump).astype(BF16)

    wait(st_z.at[pl.ds(0, 15)], sz_sem.at[1])
    final = merge(st_z)
    st_own[...] = final
    send(st_own, st_sib, sb_sem.at[0], sb_sem.at[1], dev(x, y, z, sib))

    columns = jnp.concatenate([final, jnp.zeros((120, 128), F32)], axis=0).T
    other = pl.ds(pl.multiple_of(sib * COLS, COLS), COLS)
    ours = pl.ds(pl.multiple_of(c * COLS, COLS), COLS)
    for r in range(ROUNDS):
        part = lf[r, :, :, other].reshape(128, COLS) - columns[:, r : r + 1]
        psend[r] = jnp.exp(part).astype(BF16).reshape(8, 16, COLS)
        send(
            psend.at[r], prob.at[r, :, c], pr_sem.at[0], pr_sem.at[1], dev(x, y, z, sib)
        )
    for r in range(ROUNDS):
        part = lf[r, :, :, ours].reshape(128, COLS) - columns[:, r : r + 1]
        prob[r, :, c] = jnp.exp(part).astype(BF16).reshape(8, 16, COLS)

    wait(st_sib, sb_sem.at[1])
    even = jnp.where(c == 0, st_own[...], st_sib[...])
    odd = jnp.where(c == 0, st_sib[...], st_own[...])
    both = jnp.concatenate([even, odd], axis=1)
    spots = iota((256, 256), 0)
    spots = held(lax.rem(spots, 128), lax.div(spots, 128))
    in_order = dot(both, (spots == iota((256, 256), 1)).astype(F32), HIGHEST)
    of_parent = dot(both, (spots == parent_row).astype(F32), HIGHEST)

    tree = lax.div(iota((1, 256), 1), NODES)
    limits = []
    for r in range(ROUNDS):
        limit = jnp.zeros((1, 256), jnp.int32)
        for b in range(4):
            limit = jnp.where(tree == b, accepted[r : r + 1, b : b + 1], limit)
        limits.append(limit)
    limit = jnp.concatenate(limits, axis=0).astype(F32)
    survive = depth[0:3] < limit
    lane = iota((256, 128), 1)
    in_tree = (lax.div(iota((256, 128), 0), NODES) == lax.rem(lane, 4)).astype(F32)
    counted = dot(survive.astype(F32), in_tree, HIGHEST)

    wait(pk_z.at[pl.ds(0, 15)], kz_sem.at[1])
    picks = jnp.sum(pk_z[...], axis=0)
    picked = jnp.concatenate(
        [
            jnp.concatenate([picks[2 * r : 2 * r + 1], picks[2 * r + 1 : 2 * r + 2]], axis=1)
            for r in range(ROUNDS)
        ],
        axis=0,
    )
    log_draft = picked - of_parent[0:3]
    chosen = jnp.where(survive, log_draft, 0.0)
    score = dot(chosen, in_tree, HIGHEST) / counted
    small[0:3] = in_order[3:6]
    small[3:6] = log_draft + of_parent[3:6] - math.log(typical_alpha)
    small[8:11] = jnp.concatenate([score, score], axis=1)

    wait(prob.at[:, :, 0], pr_sem.at[1])
    wait(psend, pr_sem.at[0])
    wait(st_own, sb_sem.at[0])
    wait(pk_z.at[pl.ds(0, 15)], kz_sem.at[0])
    wait(st_z.at[pl.ds(0, 15)], sz_sem.at[0])
    wait(pk_plane.at[pl.ds(0, PLANE - 1)], kp_sem.at[0])
    wait(st_plane.at[pl.ds(0, 15)], sp_sem.at[0])
    wait(lr, ls_sem.at[0])
    if GIFTS:
        wait(xg.at[pl.ds(0, len(GIFTS))], gs_sem.at[0])
    if DIRECT:
        wait(xg.at[pl.ds(0, 15), 0, pl.ds(0, DIRECT)], ds_sem.at[0])
    wait(xg.at[pl.ds(0, stepped), 0], p3s_sem.at[0])
    wait(xg.at[pl.ds(0, stepped), pl.ds(0, 2)], p2s_sem.at[0])
    wait(xg.at[pl.ds(0, stepped), 0, pl.ds(0, 3)], p1s_sem.at[0])
    wait(xg.at[pl.ds(0, count - 1), 0, 0], zs_sem.at[0])
    wait(ss_recv.at[pl.ds(0, PLANE - 1)], ss_sem.at[0])
    wait(rs_recv.at[pl.ds(0, PLANE - 1)], rs_sem.at[0])
    swap_w.wait_send()


def body(partials, norm_gain, head_weight, draft_ids, tree_parents, accepted_lengths):
    vmem = pl.BlockSpec(memory_space=pltpu.VMEM)
    hbm = pl.BlockSpec(memory_space=pltpu.HBM)
    tile = pltpu.VMEM((8, 128), F32)
    tiles = pltpu.VMEM((16, 8, 128), F32)
    one, two = pltpu.SemaphoreType.DMA((1,)), pltpu.SemaphoreType.DMA((2,))
    prob, small = pl.pallas_call(
        kernel,
        out_shape=(
            jax.ShapeDtypeStruct((ROUNDS, 8, 2, 16, COLS), BF16),
            jax.ShapeDtypeStruct((16, 256), F32),
        ),
        in_specs=[hbm] * 6,
        out_specs=(vmem, vmem),
        scratch_shapes=[
            pltpu.VMEM((ROUNDS, 4, 4096), BF16),
            pltpu.VMEM((4096,), BF16),
            pltpu.VMEM((ROUNDS, 256), jnp.int32),
            pltpu.VMEM((1, 256), jnp.int32),
            pltpu.VMEM((ROUNDS, 4), jnp.int32),
            pltpu.VMEM((2, KHALF, COLS), BF16),
            pltpu.VMEM((PLANE, 16, 128), BF16),
            pltpu.VMEM((PLANE, 16, 128), BF16),
            tile,
            pltpu.VMEM((PLANE, 8, 128), F32),
            pltpu.VMEM((Z, 4, 4, 48, 128), BF16),
            pltpu.VMEM((Z, 48, 512), F32),
            pltpu.VMEM((8, 48, 512), F32),
            pltpu.VMEM((ROUNDS, 8, 16, 512), F32),
            pltpu.VMEM((ROUNDS, 8, 16, 128), F32),
            tile,
            tiles,
            tile,
            tiles,
            tile,
            tile,
            tile,
            pltpu.VMEM((PLANE, 8, 128), F32),
            tile,
            tiles,
            pltpu.VMEM((ROUNDS, 8, 16, COLS), BF16),
            pltpu.SemaphoreType.DMA((5,)),
            pltpu.SemaphoreType.DMA((3,)),
            two,
            two,
            pltpu.SemaphoreType.DMA((Z,)),
            one,
            pltpu.SemaphoreType.DMA((Z,)),
            one,
            pltpu.SemaphoreType.DMA((Z, 2)),
            one,
            pltpu.SemaphoreType.DMA((Z,)),
            one,
            pltpu.SemaphoreType.DMA((4,)),
            one,
            one,
            pltpu.SemaphoreType.DMA((4,)),
            one,
            two,
            two,
            two,
            two,
            two,
            two,
            pltpu.SemaphoreType.REGULAR((3,)),
        ],
        compiler_params=pltpu.CompilerParams(
            collective_id=0, has_side_effects=True, vmem_limit_bytes=40 * 2**20
        ),
        name="verify",
    )(
        *(
            pltpu.with_memory_space_constraint(a, pltpu.HBM)
            for a in (
                partials,
                norm_gain,
                head_weight,
                draft_ids,
                tree_parents.reshape(1, 256),
                accepted_lengths,
            )
        )
    )
    return (
        prob.reshape(ROUNDS, 256, COLS),
        small[0:3],
        small[3:6],
        small[8:11, 0:4],
    )


def solution(mesh):
    placed = (P(None, "tensor", "vocab", None), P(), P(None, ("tensor", "vocab")), P(), P(), P())
    return jax.shard_map(
        body,
        mesh=mesh,
        in_specs=placed,
        out_specs=(P(None, None, ("tensor", "vocab")), P(), P(), P()),
        check_vma=False,
    )
```

```python
import math

import jax
import jax.numpy as jnp
from jax import lax
from jax.experimental import pallas as pl
from jax.experimental.pallas import tpu as pltpu
from jax.sharding import PartitionSpec as P

MESH = pl.DeviceIdType.MESH
HIGHEST = lax.Precision.HIGHEST
F32 = jnp.float32
BF16 = jnp.bfloat16

X = 4
Y = 4
Z = 16
PLANE = 32
KHALF = 2048
COLS = 256
ROUNDS = 3
NODES = 64
SEQ = (0, 1, -1, 3, -3, 5, -5, 4, -4, 7, -7, 8)
GIFTS = {1: (-1, 0), -1: (1, 1), 5: (-1, 2), -5: (1, 3)}
GIVEN = {2: 0, -2: 1, 6: 2, -6: 3}
GROUPS = ((0, 1, -1, 2), (-2, 3, -3, 4), (-4, 5, -5, 6), (8, 7, -7, -6))
position = {o: n for n, o in enumerate(SEQ)}
position.update({2: 1, -2: 2, 6: 5, -6: 6})
LAG = 3
DONE = 3
AHEAD = 11
DIRECT = 0
HEADS = ((4, 0, 1), (6, 1, 2), (99, 2, 3), (99, 3, 4))
FAR_FIRST = sorted(
    ((dx, dy) for dx in range(X) for dy in range(Y) if dx or dy),
    key=lambda o: abs(o[0] - 2) + abs(o[1] - 2),
)
norm_eps = 1e-06
typical_alpha = 0.3


def dot(a, b, precision=None):
    return jnp.dot(a, b, precision=precision, preferred_element_type=F32)


def iota(shape, dim):
    return lax.broadcasted_iota(jnp.int32, shape, dim)


def kernel(
    partials,
    gain,
    weight,
    draft_in,
    parents_in,
    accepted_in,
    prob,
    small,
    pbuf,
    gbuf,
    draft,
    parents,
    accepted,
    wbuf,
    rs_send,
    rs_recv,
    ss_send,
    ss_recv,
    xg,
    lp,
    lr,
    lf,
    quant,
    st_send,
    st_plane,
    st_mid,
    st_z,
    st_own,
    st_sib,
    pk_send,
    pk_plane,
    pk_mid,
    pk_z,
    psend,
    in_sem,
    w_sem,
    rs_sem,
    ss_sem,
    z_sem,
    zs_sem,
    p1_sem,
    p1s_sem,
    p2_sem,
    p2s_sem,
    p3_sem,
    p3s_sem,
    g_sem,
    gs_sem,
    ds_sem,
    l_sem,
    ls_sem,
    sp_sem,
    sz_sem,
    sb_sem,
    kp_sem,
    kz_sem,
    pr_sem,
    near_sem,
):
    t = lax.axis_index("tensor")
    v = lax.axis_index("vocab")
    x = lax.rem(v, X)
    z = lax.div(v, X)
    y = lax.div(t, 2)
    c = lax.rem(t, 2)
    sib = 1 - c

    def dev(dx, dy, dz, dc):
        return (dy * 2 + dc, dz * X + dx)

    def wait(ref, sem):
        pltpu.make_async_copy(ref, ref, sem).wait()

    def send(src, dst, ssem, rsem, device):
        pltpu.make_async_remote_copy(
            src_ref=src,
            dst_ref=dst,
            send_sem=ssem,
            recv_sem=rsem,
            device_id=device,
            device_id_type=MESH,
        ).start()

    me = c * 16 + x * Y + y

    def plane_dev(j):
        return dev(lax.div(lax.rem(j, 16), Y), lax.rem(j, Y), z, lax.div(j, 16))

    def zmate(o):
        return lax.rem(z + o + Z, Z)

    barrier = pltpu.get_barrier_semaphore()

    def greet_plane(i, carry):
        j = lax.rem(me + i, PLANE)
        pl.semaphore_signal(barrier, inc=1, device_id=plane_dev(j), device_id_type=MESH)
        return carry

    def greet_z(semaphore, distance):
        for o in (distance, -distance):
            pl.semaphore_signal(
                semaphore, inc=1, device_id=dev(x, y, zmate(o), c), device_id_type=MESH
            )

    read_partials = pltpu.make_async_copy(partials.at[:, 0], pbuf, in_sem.at[0])
    read_partials.start()
    greet_z(barrier, 1)
    lax.fori_loop(1, PLANE, greet_plane, 0)
    reads = [
        pltpu.make_async_copy(src, dst, in_sem.at[1 + i])
        for i, (src, dst) in enumerate(
            ((gain, gbuf), (draft_in, draft), (parents_in, parents), (accepted_in, accepted))
        )
    ]
    for read in reads:
        read.start()

    own_w = pltpu.make_async_copy(
        weight.at[pl.ds(c * KHALF, KHALF)], wbuf.at[c], w_sem.at[0]
    )
    own_w.start()

    read_partials.wait()
    rows = [pbuf[r].astype(F32) for r in range(ROUNDS)]
    slab = jnp.concatenate(rows + [jnp.zeros_like(rows[0])], axis=0).astype(BF16)
    for j in range(PLANE):
        rs_send[j] = slab[:, j * 128 : (j + 1) * 128]

    common = iota((128, 128), 0) & iota((128, 128), 1)
    parity = jnp.zeros((128, 128), jnp.int32)
    for bit in range(7):
        parity = parity + (lax.shift_right_logical(common, bit) & 1)
    signs = (1 - 2 * (parity & 1)).astype(F32)

    for read in reads:
        read.wait()
    gains = gbuf[...].astype(F32).reshape(PLANE, 128)
    gain_row = jnp.sum(
        jnp.where(iota((PLANE, 128), 0) == me, gains, 0.0), axis=0, keepdims=True
    )

    pl.semaphore_wait(barrier, PLANE - 1 + 2)
    greet_z(near_sem.at[0], 1)

    others = []
    for dx, dy in FAR_FIRST + [(0, 0)]:
        nx, ny = lax.rem(x + dx, X), lax.rem(y + dy, Y)
        for nc in (c, sib)[0 if dx or dy else 1 :]:
            others.append((nc * 16 + nx * Y + ny, dev(nx, ny, z, nc)))
    for j, target in others:
        send(rs_send.at[j], rs_recv.at[me], rs_sem.at[0], rs_sem.at[1], target)
    rs_recv[me] = rs_send[me]

    swap_w = pltpu.make_async_remote_copy(
        src_ref=weight.at[pl.ds(sib * KHALF, KHALF)],
        dst_ref=wbuf.at[c],
        send_sem=w_sem.at[1],
        recv_sem=w_sem.at[2],
        device_id=dev(x, y, z, sib),
        device_id_type=MESH,
    )
    pl.semaphore_wait(near_sem.at[0], 2)
    greet_z(near_sem.at[1], 2)
    wait(rs_recv.at[pl.ds(0, PLANE - 1)], rs_sem.at[1])
    swap_w.start()

    pieces = []
    for dx in range(X):
        total = jnp.zeros((16, 128), F32)
        for dy in range(Y):
            for dc in range(2):
                total = total + rs_recv[dc * 16 + dx * Y + dy].astype(F32)
        pieces.append(total)
    hidden = jnp.concatenate(
        [pieces[dx][4 * r : 4 * r + 4] for r in range(ROUNDS) for dx in range(X)],
        axis=0,
    )
    square = jnp.concatenate([hidden * hidden, jnp.zeros((80, 128), F32)], axis=0)
    ss_send[...] = jnp.broadcast_to(
        jnp.sum(square.T, axis=0, keepdims=True), (8, 128)
    )

    for j, target in others:
        send(ss_send, ss_recv.at[me], ss_sem.at[0], ss_sem.at[1], target)
    ss_recv[me] = ss_send[...]
    pl.semaphore_wait(near_sem.at[1], 2)
    greet_z(near_sem.at[2], 4)
    wait(ss_recv.at[pl.ds(0, PLANE - 1)], ss_sem.at[1])
    sums = ss_recv[0]
    for j in range(1, PLANE):
        sums = sums + ss_recv[j]
    scale = lax.rsqrt(sums[0:1] * (1.0 / 4096.0) + norm_eps)
    scale = jnp.broadcast_to(scale, (128, 128)).T[0:48]
    normed = hidden * scale * gain_row
    rotated = dot(normed, signs, HIGHEST) * (1.0 / math.sqrt(128.0))
    def order_of(n):
        return lax.rem(n + c, 2)

    def place(o, dx, dy):
        order = order_of(position[o])
        return dy + order * (dx - dy), dx + order * (dy - dx)

    def plane_step(axis_is_y, i):
        return dev(
            lax.rem(x + i * (1 - axis_is_y), X), lax.rem(y + i * axis_is_y, Y), z, c
        )

    def chunk_at(o):
        line, spot = place(o, x, y)
        return xg.at[zmate(o), line, spot]

    mine = xg.at[z, place(0, x, y)[0], place(0, x, y)[1]]
    mine[...] = rotated.astype(BF16)

    def z_start(n):
        line, spot = place(SEQ[n], x, y)
        send(
            mine,
            xg.at[z, line, spot],
            zs_sem.at[0],
            z_sem.at[n],
            dev(x, y, zmate(-SEQ[n]), c),
        )

    def across(n):
        chunk = chunk_at(SEQ[n])

        def step(i, carry):
            send(chunk, chunk, p1s_sem.at[0], p1_sem.at[n], plane_step(order_of(n), i))
            return carry

        lax.fori_loop(1, 4, step, 0)

    def along(n):
        wait(xg.at[0, 0, pl.ds(0, 3)], p1_sem.at[n])
        line = xg.at[zmate(SEQ[n]), place(SEQ[n], x, y)[0]]
        for i in range(2):
            send(
                line,
                line,
                p2s_sem.at[0],
                p2_sem.at[n, i],
                plane_step(1 - order_of(n), 1 + 2 * i),
            )

    def onward(n):
        here = place(SEQ[n], x, y)[0]
        for i in range(2):
            wait(xg.at[0, 0], p2_sem.at[n, i])
            half = xg.at[zmate(SEQ[n]), lax.rem(here + 3 - 2 * i, 4), pl.ds(2 * i, 2)]
            send(
                half,
                half,
                p3s_sem.at[0],
                p3_sem.at[n],
                plane_step(1 - order_of(n), 1 + 2 * i),
            )

    def spread(n):
        chunk = chunk_at(SEQ[n])

        def step(i, carry):
            j = lax.rem(x * Y + y + i, 16)
            target = dev(lax.div(j, Y), lax.rem(j, Y), z, c)
            send(chunk, chunk, ds_sem.at[0], p3_sem.at[n], target)
            return carry

        lax.fori_loop(1, 16, step, 0)

    def complete(n):
        wait(xg.at[0, 0] if n < stepped else xg.at[pl.ds(0, 15), 0, 0], p3_sem.at[n])
        if SEQ[n] in GIFTS:
            step, index = GIFTS[SEQ[n]]
            whole = xg.at[zmate(SEQ[n])]
            send(whole, whole, gs_sem.at[0], g_sem.at[index], dev(x, y, zmate(step), c))

    same = lax.rem(z + c, 2)

    def own_plane(g, i):
        group = GROUPS[g]
        return zmate(group[3 * i] + same * (group[1 + i] - group[3 * i]))

    def sib_plane(g, i):
        group = GROUPS[g]
        return zmate(group[1 + i] + same * (group[3 * i] - group[1 + i]))

    def head(first, last):
        offsets = [o for g in range(first, last) for o in GROUPS[g]]
        for o in offsets:
            if o in GIVEN:
                wait(xg.at[0], g_sem.at[GIVEN[o]])
        chunks = []
        for o in offsets:
            pieces = []
            for dx in range(X):
                for dy in range(Y):
                    line, spot = place(o, dx, dy)
                    pieces.append(xg[zmate(o), line, spot])
            chunks.append(jnp.concatenate(pieces, axis=1))
        lhs = jnp.concatenate(chunks, axis=0)
        for cc in range(2):
            out = dot(lhs, wbuf[cc])
            for i, o in enumerate(offsets):
                lp[zmate(o), :, cc * COLS : (cc + 1) * COLS] = out[48 * i : 48 * i + 48]
        for g in range(first, last):
            for i in range(2):
                zs = sib_plane(g, i)
                send(
                    lp.at[zs],
                    lr.at[lax.div(zs, 2)],
                    ls_sem.at[0],
                    l_sem.at[g],
                    dev(x, y, z, sib),
                )

    def stats(g):
        wait(lr.at[pl.ds(0, 2)], l_sem.at[g])
        lane = iota((48, 128), 1)
        for i in range(2):
            zs = own_plane(g, i)
            zi = lax.div(zs, 2)
            full = lp[zs] + lr[zi]
            top = jnp.max(full, axis=1, keepdims=True)
            shifted = full - top
            weights = jnp.exp(shifted)
            total = jnp.sum(weights, axis=1, keepdims=True)
            spread = jnp.sum(weights * shifted, axis=1, keepdims=True)
            log_total = jnp.log(total)
            packed = jnp.where(lane == 0, top + log_total, log_total - spread / total)
            for r in range(ROUNDS):
                lf[r, zi] = full[16 * r : 16 * r + 16]
                quant[r, zi] = packed[16 * r : 16 * r + 16]

    count = len(SEQ)
    stepped = count - DIRECT
    pl.semaphore_wait(near_sem.at[2], 2)
    for n in range(1, 1 + AHEAD):
        z_start(n)
    across(0)
    for step in range(1, count + 2 * LAG + DONE):
        if step + AHEAD < count:
            z_start(step + AHEAD)
        if step < count:
            wait(mine, z_sem.at[step])
            if step < stepped:
                across(step)
            else:
                spread(step)
        if LAG <= step < stepped + LAG:
            along(step - LAG)
        if 2 * LAG <= step < stepped + 2 * LAG:
            onward(step - 2 * LAG)
        if 2 * LAG + DONE <= step:
            complete(step - 2 * LAG - DONE)
        if step == count:
            own_w.wait()
            swap_w.wait_recv()
        for at, first, last in HEADS:
            if step == at + count:
                head(first, last)
    for at, first, last in HEADS:
        if at >= 2 * LAG + DONE:
            head(first, last)
    for g in range(len(GROUPS)):
        stats(g)

    chip = x * Y + y

    def plane_start(src, dst, sems):
        for dx, dy in FAR_FIRST:
            target = dev(lax.rem(x + dx, X), lax.rem(y + dy, Y), z, c)
            send(src, dst.at[chip], sems.at[0], sems.at[1], target)
        dst[chip] = src[...]

    def line_start(src, dst, sems):
        for o in sorted(range(1, Z), key=lambda o: abs(o - 8)):
            send(src, dst.at[z], sems.at[0], sems.at[1], dev(x, y, zmate(o), c))
        dst[z] = src[...]

    def merge(ref):
        tile = ref[...]
        part_log, part_entropy = tile[:, 0:3], tile[:, 3:6]
        top = jnp.max(part_log, axis=0)
        share = jnp.exp(part_log - top[None])
        total = jnp.sum(share, axis=0)
        log_norm = top + jnp.log(total)
        spread = jnp.sum(share * (part_entropy + (log_norm[None] - part_log)), axis=0)
        return jnp.concatenate(
            [log_norm, spread / total, jnp.zeros((2, 128), F32)], axis=0
        )

    st_send[...] = jnp.zeros((8, 128), F32)
    for r in range(ROUNDS):
        turned = quant[r].reshape(128, 128).T
        for i in range(2):
            st_send[3 * i + r : 3 * i + r + 1] = turned[i : i + 1]
    plane_start(st_send, st_plane, sp_sem)

    def held(index, core):
        return (lax.div(index, 16) * 2 + core) * 16 + lax.rem(index, 16)

    parent_row = lax.div(iota((1, 256), 1), NODES) * NODES + parents[...]
    own_parent = (held(iota((128, 256), 0), c) == parent_row).astype(F32)
    column = iota((512, 256), 0)
    column = (
        ((y * 2 + lax.div(column, COLS)) * (X * Z) + v) * COLS + lax.rem(column, COLS)
    )
    pk_send[...] = jnp.zeros((8, 128), F32)
    for r in range(ROUNDS):
        by_column = lf[r].reshape(128, 512).T
        picks = dot(by_column, own_parent, HIGHEST)
        picks = jnp.where(column == draft[r : r + 1], picks, 0.0)
        picks = jnp.sum(picks, axis=0, keepdims=True)
        pk_send[2 * r : 2 * r + 1] = picks[:, 0:128]
        pk_send[2 * r + 1 : 2 * r + 2] = picks[:, 128:256]

    def pk_start(i, carry):
        j = lax.rem(me + i, PLANE)
        send(pk_send, pk_plane.at[me], kp_sem.at[0], kp_sem.at[1], plane_dev(j))
        return carry

    lax.fori_loop(1, PLANE, pk_start, 0)
    pk_plane[me] = pk_send[...]

    wait(st_plane.at[pl.ds(0, 15)], sp_sem.at[1])
    st_mid[...] = merge(st_plane)
    line_start(st_mid, st_z, sz_sem)
    wait(pk_plane.at[pl.ds(0, PLANE - 1)], kp_sem.at[1])
    pk_mid[...] = jnp.sum(pk_plane[...], axis=0)
    line_start(pk_mid, pk_z, kz_sem)

    jump = (iota((256, 256), 0) == parent_row).astype(BF16)
    depth = jnp.broadcast_to(
        (lax.rem(iota((1, 256), 1), NODES) > 0).astype(F32), (8, 256)
    )
    for step in range(NODES.bit_length()):
        depth = depth + dot(depth.astype(BF16), jump)
        if step < NODES.bit_length() - 1:
            jump = dot(jump, jump).astype(BF16)

    wait(st_z.at[pl.ds(0, 15)], sz_sem.at[1])
    final = merge(st_z)
    st_own[...] = final
    send(st_own, st_sib, sb_sem.at[0], sb_sem.at[1], dev(x, y, z, sib))

    columns = jnp.concatenate([final, jnp.zeros((120, 128), F32)], axis=0).T
    other = pl.ds(pl.multiple_of(sib * COLS, COLS), COLS)
    ours = pl.ds(pl.multiple_of(c * COLS, COLS), COLS)
    for r in range(ROUNDS):
        part = lf[r, :, :, other].reshape(128, COLS) - columns[:, r : r + 1]
        psend[r] = jnp.exp(part).astype(BF16).reshape(8, 16, COLS)
        send(
            psend.at[r], prob.at[r, :, c], pr_sem.at[0], pr_sem.at[1], dev(x, y, z, sib)
        )
    for r in range(ROUNDS):
        part = lf[r, :, :, ours].reshape(128, COLS) - columns[:, r : r + 1]
        prob[r, :, c] = jnp.exp(part).astype(BF16).reshape(8, 16, COLS)

    wait(st_sib, sb_sem.at[1])
    even = jnp.where(c == 0, st_own[...], st_sib[...])
    odd = jnp.where(c == 0, st_sib[...], st_own[...])
    both = jnp.concatenate([even, odd], axis=1)
    spots = iota((256, 256), 0)
    spots = held(lax.rem(spots, 128), lax.div(spots, 128))
    in_order = dot(both, (spots == iota((256, 256), 1)).astype(F32), HIGHEST)
    of_parent = dot(both, (spots == parent_row).astype(F32), HIGHEST)

    tree = lax.div(iota((1, 256), 1), NODES)
    limits = []
    for r in range(ROUNDS):
        limit = jnp.zeros((1, 256), jnp.int32)
        for b in range(4):
            limit = jnp.where(tree == b, accepted[r : r + 1, b : b + 1], limit)
        limits.append(limit)
    limit = jnp.concatenate(limits, axis=0).astype(F32)
    survive = depth[0:3] < limit
    lane = iota((256, 128), 1)
    in_tree = (lax.div(iota((256, 128), 0), NODES) == lax.rem(lane, 4)).astype(F32)
    counted = dot(survive.astype(F32), in_tree, HIGHEST)

    wait(pk_z.at[pl.ds(0, 15)], kz_sem.at[1])
    picks = jnp.sum(pk_z[...], axis=0)
    picked = jnp.concatenate(
        [
            jnp.concatenate([picks[2 * r : 2 * r + 1], picks[2 * r + 1 : 2 * r + 2]], axis=1)
            for r in range(ROUNDS)
        ],
        axis=0,
    )
    log_draft = picked - of_parent[0:3]
    chosen = jnp.where(survive, log_draft, 0.0)
    score = dot(chosen, in_tree, HIGHEST) / counted
    small[0:3] = in_order[3:6]
    small[3:6] = log_draft + of_parent[3:6] - math.log(typical_alpha)
    small[8:11] = jnp.concatenate([score, score], axis=1)

    wait(prob.at[:, :, 0], pr_sem.at[1])
    wait(psend, pr_sem.at[0])
    wait(st_own, sb_sem.at[0])
    wait(pk_z.at[pl.ds(0, 15)], kz_sem.at[0])
    wait(st_z.at[pl.ds(0, 15)], sz_sem.at[0])
    wait(pk_plane.at[pl.ds(0, PLANE - 1)], kp_sem.at[0])
    wait(st_plane.at[pl.ds(0, 15)], sp_sem.at[0])
    wait(lr, ls_sem.at[0])
    if GIFTS:
        wait(xg.at[pl.ds(0, len(GIFTS))], gs_sem.at[0])
    if DIRECT:
        wait(xg.at[pl.ds(0, 15), 0, pl.ds(0, DIRECT)], ds_sem.at[0])
    wait(xg.at[pl.ds(0, stepped), 0], p3s_sem.at[0])
    wait(xg.at[pl.ds(0, stepped), pl.ds(0, 2)], p2s_sem.at[0])
    wait(xg.at[pl.ds(0, stepped), 0, pl.ds(0, 3)], p1s_sem.at[0])
    wait(xg.at[pl.ds(0, count - 1), 0, 0], zs_sem.at[0])
    wait(ss_recv.at[pl.ds(0, PLANE - 1)], ss_sem.at[0])
    wait(rs_recv.at[pl.ds(0, PLANE - 1)], rs_sem.at[0])
    swap_w.wait_send()


def body(partials, norm_gain, head_weight, draft_ids, tree_parents, accepted_lengths):
    vmem = pl.BlockSpec(memory_space=pltpu.VMEM)
    hbm = pl.BlockSpec(memory_space=pltpu.HBM)
    tile = pltpu.VMEM((8, 128), F32)
    tiles = pltpu.VMEM((16, 8, 128), F32)
    one, two = pltpu.SemaphoreType.DMA((1,)), pltpu.SemaphoreType.DMA((2,))
    prob, small = pl.pallas_call(
        kernel,
        out_shape=(
            jax.ShapeDtypeStruct((ROUNDS, 8, 2, 16, COLS), BF16),
            jax.ShapeDtypeStruct((16, 256), F32),
        ),
        in_specs=[hbm] * 6,
        out_specs=(vmem, vmem),
        scratch_shapes=[
            pltpu.VMEM((ROUNDS, 4, 4096), BF16),
            pltpu.VMEM((4096,), BF16),
            pltpu.VMEM((ROUNDS, 256), jnp.int32),
            pltpu.VMEM((1, 256), jnp.int32),
            pltpu.VMEM((ROUNDS, 4), jnp.int32),
            pltpu.VMEM((2, KHALF, COLS), BF16),
            pltpu.VMEM((PLANE, 16, 128), BF16),
            pltpu.VMEM((PLANE, 16, 128), BF16),
            tile,
            pltpu.VMEM((PLANE, 8, 128), F32),
            pltpu.VMEM((Z, 4, 4, 48, 128), BF16),
            pltpu.VMEM((Z, 48, 512), F32),
            pltpu.VMEM((8, 48, 512), F32),
            pltpu.VMEM((ROUNDS, 8, 16, 512), F32),
            pltpu.VMEM((ROUNDS, 8, 16, 128), F32),
            tile,
            tiles,
            tile,
            tiles,
            tile,
            tile,
            tile,
            pltpu.VMEM((PLANE, 8, 128), F32),
            tile,
            tiles,
            pltpu.VMEM((ROUNDS, 8, 16, COLS), BF16),
            pltpu.SemaphoreType.DMA((5,)),
            pltpu.SemaphoreType.DMA((3,)),
            two,
            two,
            pltpu.SemaphoreType.DMA((Z,)),
            one,
            pltpu.SemaphoreType.DMA((Z,)),
            one,
            pltpu.SemaphoreType.DMA((Z, 2)),
            one,
            pltpu.SemaphoreType.DMA((Z,)),
            one,
            pltpu.SemaphoreType.DMA((4,)),
            one,
            one,
            pltpu.SemaphoreType.DMA((4,)),
            one,
            two,
            two,
            two,
            two,
            two,
            two,
            pltpu.SemaphoreType.REGULAR((3,)),
        ],
        compiler_params=pltpu.CompilerParams(
            collective_id=0, has_side_effects=True, vmem_limit_bytes=40 * 2**20
        ),
        name="verify",
    )(
        *(
            pltpu.with_memory_space_constraint(a, pltpu.HBM)
            for a in (
                partials,
                norm_gain,
                head_weight,
                draft_ids,
                tree_parents.reshape(1, 256),
                accepted_lengths,
            )
        )
    )
    return (
        prob.reshape(ROUNDS, 256, COLS),
        small[0:3],
        small[3:6],
        small[8:11, 0:4],
    )


def solution(mesh):
    placed = (P(None, "tensor", "vocab", None), P(), P(None, ("tensor", "vocab")), P(), P(), P())
    return jax.shard_map(
        body,
        mesh=mesh,
        in_specs=placed,
        out_specs=(P(None, None, ("tensor", "vocab")), P(), P(), P()),
        check_vma=False,
    )
```
